32 devices in a mesh: ka: 4 (over x, core), ta: 8 (over z, y).
Axes of the slice: x: 2, y: 2, z: 4, core: 2. Of those that a mesh axis runs over, the one named last changes fastest.
Arguments:
- history: bfloat16 [512, 16, 32768], P('ta', None, 'ka'), may hold values from -6 to 6
- energy: float32 [512, 2, 32768], P('ta', None, 'ka'), may hold values from -0.5 to 0.5
- kernel: float32 [512, 16, 16], P('ta'), may hold values from -0.0625 to 0.0625
- newest: int32 [1], replicated, may hold values from 0 to 511
- current: float32 [16, 32768], P(None, 'ka'), may hold values from -6 to 6
- step_energy: float32 [2, 32768], P(None, 'ka'), may hold values from -3.140625 to 3.140625
Outputs:
- new_slice: float32 [16, 32768], P(None, 'ka')
- new_history: bfloat16 [512, 16, 32768], P('ta', None, 'ka')
The draws below stay inside these ranges and needn't reach their ends.
Inputs may be any that keep to these rules, and one draw needn't show every extreme that they name: Stored steps form a circular buffer; the slot after the newest holds the oldest step.
All inputs are finite; a program needn't handle non-finite values.
Results may differ from the reference program's by a relative error of at most 0.001.
Values sent between devices are 32-bit elements; how exact they have to be, the bound alone decides.
No kernel may reach another device: no remote copies, remote signals or barrier semaphores. Data moves between devices by JAX's collectives and lax.ppermute only.
A program may use at most 128 MiB of HBM per device.

```python
import jax
import jax.numpy as jnp
from jax import lax

K = 32768
NT = 512


def block_levels(own_key, extent, split, low, largest):
    def one(axis_at, blocks):
        draws = jax.random.uniform(jax.random.fold_in(jax.random.fold_in(own_key, 6), axis_at), (blocks,), jnp.float32, low / len(split), largest / len(split))
        return jnp.repeat(jnp.exp(draws), extent[axis_at] // blocks).reshape((-1,) + (1,) * (len(extent) - axis_at - 1))

    gain = one(*split[0])
    for cut in split[1:]:
        gain = gain * one(*cut)
    return gain


def normal_values(stream_key, shape, deviation, most, pieces=(), kind=jnp.bfloat16):
    entries = jax.random.normal(stream_key, shape, jnp.float32) * deviation
    if len(pieces) > 0:
        entries = block_levels(stream_key, shape, pieces, -0.22, 0.18) * entries
    return jnp.clip(entries, min=-most, max=most).astype(kind)


def setup_inputs(seed: int = 0) -> dict:
    splits = jax.random.split(jax.random.key(seed), 7)
    return {
        "history": normal_values(splits[0], (NT, 16, K), 1.0, 6.0, ((0, 8), (2, 4))),
        "energy": jnp.clip(jax.random.uniform(splits[1], (NT, 2, K), jnp.float32, -0.5, 0.5) * block_levels(splits[1], (NT, 2, K), ((0, 8), (2, 4)), -0.4, 0.0), -0.5, 0.5),
        "kernel": normal_values(splits[2], (NT, 16, 16), (16 * NT) ** -0.5, 0.0625, ((0, 8),), jnp.float32),
        "newest": jax.random.randint(splits[3], (1,), 0, NT).astype(jnp.int32),
        "current": normal_values(splits[4], (16, K), 1.0, 6.0, ((1, 4),), jnp.float32),
        "step_energy": jnp.clip(jax.random.uniform(splits[5], (2, K), jnp.float32, -3.140625, 3.140625), -3.140625, 3.140625),
    }


def rotate(values, angles):
    leading = angles.shape[:-2]
    columns = angles.shape[-1]
    spread_angles = jnp.broadcast_to(angles[..., None, :, None, :], leading + (2, 2, 2, columns)).reshape(leading + (8, columns))
    cosine = jnp.cos(spread_angles)
    sine_part = jnp.sin(spread_angles)
    real_part = values[..., :8, :]
    imag_part = values[..., 8:, :]
    return jnp.concatenate([cosine * real_part + sine_part * imag_part, cosine * imag_part - sine_part * real_part], axis=-2)


def reference(history, energy, kernel, newest, current, step_energy):
    latest = newest[0]
    order_slots = ((latest - jnp.arange(NT, dtype=jnp.int32)) % NT).astype(jnp.int32)
    ordered = jnp.take(energy, order_slots, axis=0)
    cumulative = jnp.cumsum(ordered, axis=0)
    phases = jnp.take(cumulative, order_slots, axis=0)
    start_slice = rotate(current, step_energy)

    def predictor_step(carry, items):
        stored, phase_row, weights = items
        turned = rotate(stored.astype(jnp.float32), phase_row)
        return carry + jnp.dot(weights, turned, precision=lax.Precision.HIGHEST), None

    memory_pred, unused = lax.scan(predictor_step, jnp.zeros((16, K), jnp.float32), (history, phases, kernel))
    predicted = start_slice + memory_pred

    def corrector_step(carry, items):
        stored, phase_row, weights = items
        turned = rotate(stored.astype(jnp.float32), phase_row)
        intersection = 0.25 * jnp.sum(predicted * turned, axis=0)
        vertex = 1.0 / (1.0 + intersection * intersection)
        return carry + jnp.dot(weights, turned * vertex[None, :], precision=lax.Precision.HIGHEST), None

    memory_corr, unused_two = lax.scan(corrector_step, jnp.zeros((16, K), jnp.float32), (history, phases, kernel))
    new_slice = start_slice + 0.5 * (memory_pred + memory_corr)
    target = ((latest + 1) % NT).astype(jnp.int32)
    new_history = lax.dynamic_update_slice(history, new_slice.astype(jnp.bfloat16)[None], (target, jnp.int32(0), jnp.int32(0)))
    return new_slice, new_history
```

```python
import functools

import jax
import jax.numpy as jnp
import numpy as np
from jax import lax
from jax.experimental import pallas as pl
from jax.experimental.pallas import tpu as pltpu
from jax.sharding import PartitionSpec as P

LANES = 128
WIDE = 4 * LANES
CHUNK = 1024
VM = pl.BlockSpec(memory_space=pltpu.VMEM)
SM = pl.BlockSpec(memory_space=pltpu.SMEM)
HB = pl.BlockSpec(memory_space=pl.ANY)
SIN = (1.41420874, -0.235676110, 0.0117467684, -2.59660918e-4)
COS = (1.41421350, -0.707105432, 0.0589211807, -1.95919014e-3, 3.27400865e-5)
BF = jnp.bfloat16
F32 = jnp.float32


def group_of(steps):
    return 16 if steps % 16 == 0 else 8


def half_angle_sincos(half):
    turns = jnp.round(half * (1.0 / np.pi))
    u = half - turns * np.pi
    q = u * u
    z = u * (SIN[0] + q * (SIN[1] + q * (SIN[2] + q * SIN[3])))
    c = COS[0] + q * (COS[1] + q * (COS[2] + q * (COS[3] + q * COS[4])))
    return z * c, 1.0 - z * z


def trig_kernel(tri_ref, energy_ref, cos_ref, sin_ref, held, sems):
    steps, columns = cos_ref.shape[1:]
    chunk = min(CHUNK, columns)
    count = columns // chunk

    def copy(j, a):
        lanes = pl.ds(j * chunk, chunk)
        return pltpu.make_async_copy(
            energy_ref.at[:, a, lanes], held.at[a, :, lanes], sems.at[j, a]
        )

    for j in range(count):
        for a in range(2):
            copy(j, a).start()
    for j in range(count):
        for a in range(2):
            copy(j, a).wait()
        for n in range(chunk // WIDE):
            lanes = slice(j * chunk + n * WIDE, j * chunk + (n + 1) * WIDE)
            for a in range(2):
                e = held[a, :, lanes]
                top = e.astype(BF)
                rest = e - top.astype(F32)
                mid = rest.astype(BF)
                low = (rest - mid.astype(F32)).astype(BF)
                half = jnp.dot(
                    tri_ref[...],
                    jnp.concatenate([top, mid, low], axis=0),
                    preferred_element_type=F32,
                )
                s, c = half_angle_sincos(half)
                cos_ref[a, :, lanes] = c
                sin_ref[a, :, lanes] = s


def trig(energy):
    steps, _, columns = energy.shape
    tri = 0.5 * np.triu(np.ones((steps, steps), np.float32))
    tri = jnp.asarray(np.concatenate([tri] * 3, axis=1), BF)
    size = (2, steps, columns)
    return pl.pallas_call(
        trig_kernel,
        in_specs=[VM, HB],
        out_specs=[VM, VM],
        out_shape=[jax.ShapeDtypeStruct(size, F32)] * 2,
        scratch_shapes=[
            pltpu.VMEM(size, F32),
            pltpu.SemaphoreType.DMA((columns // min(CHUNK, columns), 2)),
        ],
        compiler_params=pltpu.CompilerParams(vmem_limit_bytes=32 << 20),
        cost_estimate=pl.CostEstimate(
            flops=40 * size[0] * size[1] * size[2], bytes_accessed=4 * 3 * size[0] * size[1] * size[2], transcendentals=0
        ),
        name="trig",
    )(tri, energy)


def permutation(group):
    rows = 16 * group
    p = np.zeros((rows, rows), np.float32)
    for tile in range(2):
        for c in range(8):
            for g in range(group // 8):
                for s in range(8):
                    p[((tile * 8 + c) * (group // 8) + g) * 8 + s, ((8 * g + s) * 2 + tile) * 8 + c] = 1
    return jnp.asarray(p, BF)


def kernel_rows(kernel):
    steps = kernel.shape[0]
    group = group_of(steps)
    k = kernel.reshape(steps // group, group // 8, 8, 16, 16).transpose(0, 3, 1, 4, 2)
    k = k.reshape(steps // group, 16, 16 * group)
    top = lax.reduce_precision(k, 8, 7)
    return jnp.concatenate([top, k - top], axis=1).astype(BF)


def mix_kernel(correct, copies, steps, group, sc_ref, perm_ref, k_ref, h_ref, cos_ref, sin_ref, off_ref, *rest):
    rest = list(rest)
    if correct:
        start_ref, pred_ref, out_ref, held, in_sems, wide_ref = rest
    else:
        if copies:
            rest.pop(0)
        out_ref, new_ref, held, in_sems, out_sems = rest
    columns = out_ref.shape[-1]
    chunk = min(CHUNK, columns)
    count = columns // chunk
    tiles = chunk // LANES
    blocks = group // 8
    edge = sc_ref[1]
    base = sc_ref[0] * columns

    def rows_at(j):
        return pl.ds(pl.multiple_of((sc_ref[0] * (columns // LANES) + j * tiles) * 8, 16), tiles * 8)

    def copy_in(j):
        here = pl.ds(pl.multiple_of(j * tiles * 8, 16), tiles * 8)
        return pltpu.make_async_copy(h_ref.at[:, :, rows_at(j)], held.at[:, :, here], in_sems.at[j])

    def copy_out(j):
        here = pl.ds(pl.multiple_of(j * tiles * 8, 16), tiles * 8)
        return pltpu.make_async_copy(held.at[:, :, here], new_ref.at[:, :, rows_at(j)], out_sems.at[j])

    for j in range(count):
        copy_in(j).start()

    def body(j, n):
        first = j * chunk + n * WIDE
        row = pl.multiple_of(j * tiles * 8 + n * 32, 16)
        local = [pl.ds(pl.multiple_of(first + LANES * t, LANES), LANES) for t in range(4)]
        whole = [pl.ds(pl.multiple_of(base + first + LANES * t, LANES), LANES) for t in range(4)]

        def both(ref, *index):
            return lambda t: jnp.concatenate([ref[(*index, whole[t])], ref[(*index, whole[t + 2])]], axis=-1)

        if correct:
            full = 0.25 * (
                start_ref[:, pl.ds(pl.multiple_of(base + first, LANES), WIDE)]
                + pred_ref[:, pl.ds(pl.multiple_of(first, LANES), WIDE)]
            )
            for c in range(16):
                wide_ref[c] = jnp.broadcast_to(full[c : c + 1], (8, WIDE))
        turn = [
            [
                [both(off_ref, part, slice(2 * side + a, 2 * side + a + 1))(t) for a in range(2)]
                for side in range(2)
            ]
            for part in range(2)
            for t in range(2)
        ]
        sums = [jnp.zeros((32, 2 * LANES), F32) for _ in range(2)]
        lows = [jnp.zeros((16, 2 * LANES), F32) for _ in range(2)]
        for i in range(steps // group):
            moved = []
            for part in range(2):
                h = jnp.concatenate(
                    [
                        held[i * group : (i + 1) * group, part, pl.ds(pl.multiple_of(row + 16 * p, 16), 16)].reshape(
                            16 * group, LANES
                        )
                        for p in range(2)
                    ],
                    axis=1,
                )
                moved.append(jnp.dot(perm_ref[...], h, preferred_element_type=F32))
            for t in range(2):
                parts = []
                for g in range(blocks):
                    s0 = i * group + 8 * g
                    after = lax.broadcasted_iota(jnp.int32, (8, 2 * LANES), 0) + s0 > edge
                    angle = []
                    for a in range(2):
                        c = both(cos_ref, a, slice(s0, s0 + 8))(t)
                        s = both(sin_ref, a, slice(s0, s0 + 8))(t)
                        co = jnp.where(after, turn[t][1][a], turn[t][0][a])
                        so = jnp.where(after, turn[2 + t][1][a], turn[2 + t][0][a])
                        angle.append((c * co - s * so, s * co + c * so))
                    real, imag = [], []
                    for e in range(8):
                        c, s = angle[(e >> 1) & 1]
                        at = ((t * 8 + e) * blocks + g) * 8
                        x = moved[0][at : at + 8]
                        y = moved[1][at : at + 8]
                        real.append(c * x + s * y)
                        imag.append(c * y - s * x)
                    turned = real + imag
                    if correct:
                        terms = [
                            turned[c]
                            * jnp.concatenate(
                                [
                                    wide_ref[c, :, t * LANES : (t + 1) * LANES],
                                    wide_ref[c, :, (t + 2) * LANES : (t + 3) * LANES],
                                ],
                                axis=-1,
                            )
                            for c in range(16)
                        ]
                        while len(terms) > 1:
                            terms = [terms[m] + terms[m + 1] for m in range(0, len(terms), 2)]
                        vertex = 1.0 / (1.0 + terms[0] * terms[0])
                        turned = [vertex * x for x in turned]
                    parts += turned
                x = jnp.concatenate(parts, axis=0)
                top = x.astype(BF)
                low = (x - top.astype(F32)).astype(BF)
                sums[t] = sums[t] + jnp.dot(k_ref[i], top, preferred_element_type=F32)
                lows[t] = lows[t] + jnp.dot(k_ref[i, :16], low, preferred_element_type=F32)
        for t in range(2):
            total = (sums[t][:16] + sums[t][16:]) + lows[t]
            out_ref[:, local[t]] = total[:, :LANES]
            out_ref[:, local[t + 2]] = total[:, LANES:]

    @pl.loop(0, count)
    def _(j):
        copy_in(j).wait()
        if not correct:
            copy_out(j).start()
        for n in range(chunk // WIDE):
            body(j, n)

    if not correct:
        for j in range(count):
            copy_out(j).wait()


def mix(side, edge, weights, stored, cosine, sine, off, start=None, pred=None, new=None):
    steps = cosine.shape[1]
    columns = cosine.shape[2] // 2
    group = group_of(steps)
    correct = pred is not None
    copies = new is not None
    chunk = min(CHUNK, columns)
    count = columns // chunk
    args = [jnp.stack([side, edge]).astype(jnp.int32), permutation(group), weights, stored, cosine, sine, off]
    specs = [SM, VM, VM, HB, VM, VM, VM]
    out_shape = [jax.ShapeDtypeStruct((16, columns), F32)]
    out_specs = [VM]
    scratch = [
        pltpu.VMEM((steps, 2, columns // 16, LANES), BF),
        pltpu.SemaphoreType.DMA((count,)),
    ]
    aliases = {}
    if correct:
        args += [start, pred]
        specs += [VM, VM]
        scratch.append(pltpu.VMEM((16, 8, WIDE), F32))
    else:
        if copies:
            aliases = {len(args): 1}
            args.append(new)
            specs.append(HB)
        out_shape.append(jax.ShapeDtypeStruct(stored.shape, stored.dtype))
        out_specs.append(HB)
        scratch.append(pltpu.SemaphoreType.DMA((count,)))
    size = steps * 16 * columns
    return pl.pallas_call(
        functools.partial(mix_kernel, correct, copies, steps, group),
        in_specs=specs,
        out_specs=out_specs,
        out_shape=out_shape,
        scratch_shapes=scratch,
        input_output_aliases=aliases,
        compiler_params=pltpu.CompilerParams(vmem_limit_bytes=36 << 20),
        cost_estimate=pl.CostEstimate(flops=200 * size, bytes_accessed=(2 if correct else 4) * size, transcendentals=0),
        name="correct" if correct else "predict",
    )(*args)


def place_kernel(sc_ref, old_ref, slice_ref, new_ref, held, sem):
    held[...] = slice_ref[...].astype(BF)

    @pl.when(sc_ref[0] == 1)
    def _():
        copy = pltpu.make_async_copy(held, new_ref.at[sc_ref[1]], sem)
        copy.start()
        copy.wait()


def place(own, slot, new, corrected):
    return pl.pallas_call(
        place_kernel,
        in_specs=[SM, HB, VM],
        out_specs=HB,
        out_shape=jax.ShapeDtypeStruct(new.shape, new.dtype),
        scratch_shapes=[pltpu.VMEM(new.shape[1:], BF), pltpu.SemaphoreType.DMA],
        input_output_aliases={1: 0},
        name="place",
    )(jnp.stack([own, slot]).astype(jnp.int32), new, corrected)


def tiled(x):
    lead, columns = x.shape[:-2], x.shape[-1]
    x = x.reshape(*lead, 2, 8, columns // LANES, LANES)
    return jnp.swapaxes(x, -3, -2).reshape(*lead, 2, columns // 16, LANES)


def untiled(x):
    lead, rows = x.shape[:-3], x.shape[-2]
    x = jnp.swapaxes(x.reshape(*lead, 2, rows // 8, 8, LANES), -3, -2)
    return x.reshape(*lead, 16, rows * 16)


def rotate(values, angles):
    columns = angles.shape[-1]
    spread = jnp.broadcast_to(angles[None, :, None, :], (2, 2, 2, columns)).reshape(8, columns)
    c, s = jnp.cos(spread), jnp.sin(spread)
    real, imag = values[:8], values[8:]
    return jnp.concatenate([c * real + s * imag, c * imag - s * real], axis=0)


def on_device(history, energy, kernel, newest, current, step_energy):
    steps, _, columns = history.shape
    count = lax.axis_size("ta")
    place_here = lax.axis_index("ta")
    bits = count.bit_length() - 1
    half = columns // 2
    latest = newest[0]
    owner = lax.div(latest, steps)
    edge = latest - place_here * steps
    side = place_here & 1
    other = 1 - side

    def swap(x, mask):
        return lax.ppermute(x, "ta", [(i, i ^ mask) for i in range(count)])

    masks = [2] + [6 if t == 2 else 1 << t for t in range(2, bits)]
    split = (place_here >> 1 ^ place_here >> 2) & 1

    slots = jnp.arange(steps, dtype=jnp.int32)
    early = jnp.sum(jnp.where((slots <= edge)[:, None, None], energy, 0.0), axis=0)
    late = jnp.sum(jnp.where((slots > edge)[:, None, None], energy, 0.0), axis=0)
    mine = place_here == owner
    value = jnp.where(mine, early, early + late)

    cosine, sine = trig(energy)

    total, ahead = value, jnp.zeros_like(value)
    for t in range(bits):
        mask = 6 if t == 2 else 1 << t
        got = swap(total, mask)
        here, there = place_here >> t, owner >> t
        upper = (here & 1) == 1
        partner = here ^ 1
        counted_low = ~((there == here) & (place_here < owner))
        counted_high = (there == partner) | ((there == here) & (place_here >= owner))
        ahead = ahead + jnp.where(jnp.where(upper, counted_high, counted_low), got, 0.0)
        low_group = jnp.where(upper, partner, here)
        total = jnp.where(there == low_group, jnp.where(upper, got, total), total + got)
    off = jnp.concatenate(
        [jnp.where(mine, -late, ahead), jnp.where(mine, ahead + value, ahead)], axis=0
    )
    off = jnp.stack([jnp.cos(off), jnp.sin(off)])

    weights = kernel_rows(kernel)
    stored = tiled(history)
    start = rotate(current, step_energy)

    def inner_sum(x):
        first = split == 0
        keep = jnp.where(first, x[:8], x[8:])
        send = jnp.where(first, x[8:], x[:8])
        keep = keep + swap(send, masks[0])
        for mask in masks[1:]:
            keep = keep + swap(keep, mask)
        rest = swap(keep, masks[0])
        return jnp.concatenate([jnp.where(first, keep, rest), jnp.where(first, rest, keep)], axis=0)

    part_other, new = mix(other, edge, weights, stored, cosine, sine, off)
    from_partner = swap(part_other, 1)
    part_own, new = mix(side, edge, weights, stored, cosine, sine, off, new=new)
    pred_own = inner_sum(part_own + from_partner)
    pred_other = swap(pred_own, 1)
    (corr_own,) = mix(side, edge, weights, stored, cosine, sine, off, start, pred_own)
    from_partner = swap(corr_own, 1)
    (corr_other,) = mix(other, edge, weights, stored, cosine, sine, off, start, pred_other)
    corr = inner_sum(corr_other + from_partner)
    start_other = jnp.where(side == 0, start[:, half:], start[:, :half])
    new_other = start_other + 0.5 * (pred_other + corr)
    new_own = swap(new_other, 1)
    corrected = jnp.concatenate(
        [jnp.where(side == 0, new_own, new_other), jnp.where(side == 0, new_other, new_own)], axis=1
    )
    target = lax.rem(latest + 1, steps * count)
    own = lax.div(target, steps) == place_here
    new = place(own, lax.rem(target, steps), new, tiled(corrected))
    return corrected, untiled(new)


def solution(mesh):
    return jax.shard_map(
        on_device,
        mesh=mesh,
        in_specs=(
            P("ta", None, "ka"),
            P("ta", None, "ka"),
            P("ta", None, None),
            P(),
            P(None, "ka"),
            P(None, "ka"),
        ),
        out_specs=(P(None, "ka"), P("ta", None, "ka")),
        check_vma=False,
    )
```

```python
import functools

import jax
import jax.numpy as jnp
import numpy as np
from jax import lax
from jax.experimental import pallas as pl
from jax.experimental.pallas import tpu as pltpu
from jax.sharding import PartitionSpec as P

LANES = 128
WIDE = 4 * LANES
CHUNK = 1024
VM = pl.BlockSpec(memory_space=pltpu.VMEM)
SM = pl.BlockSpec(memory_space=pltpu.SMEM)
HB = pl.BlockSpec(memory_space=pltpu.HBM)
SIN = (1.41420874, -0.235676110, 0.0117467684, -2.59660918e-4)
COS = (1.41421350, -0.707105432, 0.0589211807, -1.95919014e-3, 3.27400865e-5)
BF = jnp.bfloat16
F32 = jnp.float32
SELF = [slice(t * LANES, (t + 1) * LANES) for t in range(4)]


GROUP = 8


def double_sincos(u):
    q = u * u
    z = u * (SIN[0] + q * (SIN[1] + q * (SIN[2] + q * SIN[3])))
    c = COS[0] + q * (COS[1] + q * (COS[2] + q * (COS[3] + q * COS[4])))
    return z * c, 1.0 - z * z


def half_angle_sincos(half):
    return double_sincos(half - jnp.round(half * (1.0 / np.pi)) * np.pi)


def sincos(angle):
    half = 0.5 * angle
    turns = jnp.round(half * (1.0 / np.pi))
    return double_sincos((half - turns * 3.140625) - turns * 9.67653589793e-4)


def pieces_of(steps):
    return 4 if steps % 4 == 0 else 1


def totals_kernel(edge_ref, energy_ref, value_ref, late_ref, held, sems):
    steps = energy_ref.shape[0]
    pieces = pieces_of(steps)
    each = steps // pieces
    edge = edge_ref[0]

    def copy(p):
        part = pl.ds(p * each, each)
        return pltpu.make_async_copy(energy_ref.at[part], held.at[part], sems.at[p])

    for p in range(pieces):
        copy(p).start()
    total = jnp.zeros(value_ref.shape, F32)
    late = jnp.zeros(value_ref.shape, F32)
    for p in range(pieces):
        copy(p).wait()
        for s in range(p * each, (p + 1) * each):
            e = held[s]
            total = total + e
            late = late + e * (s > edge).astype(F32)
    mine = (edge >= 0) & (edge < steps)
    value_ref[...] = jnp.where(mine, total - late, total)
    late_ref[...] = late


def totals(edge, energy):
    steps, _, columns = energy.shape
    rows = columns // (LANES // 2)
    view = energy.reshape(steps, 2, columns // LANES, LANES).transpose(0, 2, 1, 3).reshape(steps, rows, LANES)
    return pl.pallas_call(
        totals_kernel,
        in_specs=[SM, HB],
        out_specs=[VM, VM],
        out_shape=[jax.ShapeDtypeStruct((rows, LANES), F32)] * 2,
        scratch_shapes=[pltpu.VMEM(view.shape, F32), pltpu.SemaphoreType.DMA((pieces_of(steps),))],
        compiler_params=pltpu.CompilerParams(vmem_limit_bytes=54 << 20),
        cost_estimate=pl.CostEstimate(flops=4 * energy.size, bytes_accessed=4 * energy.size, transcendentals=0),
        name="totals",
    )(jnp.reshape(edge, (1,)).astype(jnp.int32), view)


def trig_kernel(tri_ref, energy_ref, waves_ref, held, made, in_sems, out_sems):
    columns = held.shape[-1]
    chunk = min(CHUNK, columns)
    count = columns // chunk

    def copy_in(j, a):
        lanes = pl.ds(j * chunk, chunk)
        return pltpu.make_async_copy(energy_ref.at[:, a, lanes], held.at[a, :, lanes], in_sems.at[j, a])

    def copy_out(j):
        lanes = pl.ds(j * chunk, chunk)
        return pltpu.make_async_copy(made.at[:, :, :, lanes], waves_ref.at[:, :, :, lanes], out_sems.at[j])

    for j in range(count):
        for a in range(2):
            copy_in(j, a).start()
    for j in range(count):
        for a in range(2):
            copy_in(j, a).wait()
        for n in range(chunk // WIDE):
            lanes = slice(j * chunk + n * WIDE, j * chunk + (n + 1) * WIDE)
            for a in range(2):
                e = held[a, :, lanes]
                top = e.astype(BF)
                rest = e - top.astype(F32)
                mid = rest.astype(BF)
                low = (rest - mid.astype(F32)).astype(BF)
                half = jnp.dot(
                    tri_ref[...],
                    jnp.concatenate([top, mid, low], axis=0),
                    preferred_element_type=F32,
                )
                s, c = half_angle_sincos(half)
                made[0, a, :, lanes] = c
                made[1, a, :, lanes] = s
        copy_out(j).start()
    for j in range(count):
        copy_out(j).wait()


def trig(energy):
    steps, _, columns = energy.shape
    tri = 0.5 * np.triu(np.ones((steps, steps), np.float32))
    tri = jnp.asarray(np.concatenate([tri] * 3, axis=1), BF)
    count = columns // min(CHUNK, columns)
    size = (2, 2, steps, columns)
    return pl.pallas_call(
        trig_kernel,
        in_specs=[VM, HB],
        out_specs=HB,
        out_shape=jax.ShapeDtypeStruct(size, F32),
        scratch_shapes=[
            pltpu.VMEM(size[1:], F32),
            pltpu.VMEM(size, F32),
            pltpu.SemaphoreType.DMA((count, 2)),
            pltpu.SemaphoreType.DMA((count,)),
        ],
        compiler_params=pltpu.CompilerParams(vmem_limit_bytes=54 << 20),
        cost_estimate=pl.CostEstimate(flops=40 * energy.size, bytes_accessed=12 * energy.size, transcendentals=0),
        name="trig",
    )(tri, energy)


def permutation(group):
    rows = 16 * group
    p = np.zeros((rows, rows), np.float32)
    for tile in range(2):
        for c in range(8):
            for g in range(group // 8):
                for s in range(8):
                    p[((tile * 8 + c) * (group // 8) + g) * 8 + s, ((8 * g + s) * 2 + tile) * 8 + c] = 1
    return jnp.asarray(p, BF)


def kernel_rows(kernel):
    steps = kernel.shape[0]
    group = GROUP
    k = kernel.reshape(steps // group, group // 8, 8, 16, 16).transpose(0, 3, 1, 4, 2)
    k = k.reshape(steps // group, 16, 16 * group)
    top = lax.reduce_precision(k, 8, 7)
    return jnp.concatenate([top, k - top], axis=1).astype(BF)


def predict_kernel(steps, group, sc_ref, perm_ref, k_ref, h_ref, waves_ref, off_ref, out_ref, turned_ref, held, in_sems, waves, wave_sems, kept, out_sems):
    columns = out_ref.shape[-1]
    chunk = kept.shape[-1]
    count = columns // chunk
    tiles = chunk // LANES
    blocks = group // 8
    edge = sc_ref[1]
    base = sc_ref[0] * columns

    def copy_in(j):
        there = pl.ds(pl.multiple_of((sc_ref[0] * (columns // LANES) + j * tiles) * 8, 16), tiles * 8)
        here = pl.ds(pl.multiple_of(j * tiles * 8, 16), tiles * 8)
        return pltpu.make_async_copy(h_ref.at[:, :, there], held.at[:, :, here], in_sems.at[j])

    def copy_out(j):
        there = pl.ds(pl.multiple_of(j * chunk, chunk), chunk)
        return pltpu.make_async_copy(kept.at[j % 2], turned_ref.at[:, there], out_sems.at[j % 2])

    def copy_waves(j):
        there = pl.ds(pl.multiple_of(base + j * chunk, chunk), chunk)
        here = pl.ds(pl.multiple_of(j * chunk, chunk), chunk)
        return pltpu.make_async_copy(waves_ref.at[:, :, :, there], waves.at[:, :, :, here], wave_sems.at[j])

    for j in range(count):
        copy_in(j).start()
        copy_waves(j).start()

    def spans(j, n):
        first = j * chunk + n * WIDE
        local = [pl.ds(pl.multiple_of(first + LANES * t, LANES), LANES) for t in range(4)]
        return local

    def pair(part, a, s0, local, t):
        rows = slice(s0, s0 + 8)
        return jnp.concatenate([waves[part, a, rows, local[t]], waves[part, a, rows, local[t + 2]]], axis=-1)

    def off_row(part, later_side, j, n, t, a):
        row = 2 * ((sc_ref[0] * (columns // LANES)) + j * tiles + 4 * n + t) + a
        return jnp.concatenate(
            [off_ref[part, later_side, pl.ds(row, 1)], off_ref[part, later_side, pl.ds(row + 4, 1)]], axis=-1
        )

    def move(j, n, i):
        row = pl.multiple_of(j * tiles * 8 + n * 32, 16)
        moved = []
        for part in range(2):
            h = [
                held[i * group : (i + 1) * group, part, pl.ds(pl.multiple_of(row + 16 * p, 16), 16)].reshape(
                    16 * group, LANES
                )
                for p in range(2)
            ]
            moved.append(jnp.dot(perm_ref[...], jnp.concatenate(h, axis=1), preferred_element_type=F32))
        return moved

    def turned_rows(local, i, t, g, moved, turn):
        s0 = i * group + 8 * g
        after = lax.broadcasted_iota(jnp.int32, (8, 2 * LANES), 0) + s0 > edge
        angle = []
        for a in range(2):
            c = pair(0, a, s0, local, t)
            s = pair(1, a, s0, local, t)
            co = jnp.where(after, turn[t][1][a], turn[t][0][a])
            so = jnp.where(after, turn[2 + t][1][a], turn[2 + t][0][a])
            angle.append((c * co - s * so, s * co + c * so))
        real, imag = [], []
        for e in range(8):
            c, s = angle[(e >> 1) & 1]
            at = ((t * 8 + e) * blocks + g) * 8
            x = moved[0][at : at + 8]
            y = moved[1][at : at + 8]
            real.append(c * x + s * y)
            imag.append(c * y - s * x)
        return real + imag

    def work(j):
        items = [(n, i) for n in range(chunk // WIDE) for i in range(steps // group)]
        sums = {}
        buf = j % 2

        def contract(n, i, ready):
            for t in range(2):
                top, low = ready[t]
                first = jnp.dot(k_ref[i], top, preferred_element_type=F32)
                second = jnp.dot(k_ref[i, :16], low, preferred_element_type=F32)
                if i > 0:
                    first, second = sums[n, t][0] + first, sums[n, t][1] + second
                sums[n, t] = first, second
                if i == steps // group - 1:
                    total = (first[:16] + first[16:]) + second
                    local = spans(j, n)
                    out_ref[:, local[t]] = total[:, :LANES]
                    out_ref[:, local[t + 2]] = total[:, LANES:]

        moved = move(j, *items[0])
        waiting = None
        for at, (n, i) in enumerate(items):
            if waiting is not None:
                contract(*waiting)
            later = move(j, *items[at + 1]) if at + 1 < len(items) else None
            local = spans(j, n)
            if i == 0:
                turn = [
                    [[off_row(part, later_side, j, n, t, a) for a in range(2)] for later_side in range(2)]
                    for part in range(2)
                    for t in range(2)
                ]
            ready = []
            rows = slice(i * 16 * group, (i + 1) * 16 * group)
            for t in range(2):
                x = jnp.concatenate(
                    [row for g in range(blocks) for row in turned_rows(local, i, t, g, moved, turn)], axis=0
                )
                kept[buf, rows, n * WIDE + t * LANES : n * WIDE + (t + 1) * LANES] = x[:, :LANES]
                kept[buf, rows, n * WIDE + (t + 2) * LANES : n * WIDE + (t + 3) * LANES] = x[:, LANES:]
                top = x.astype(BF)
                ready.append((top, (x - top.astype(F32)).astype(BF)))
            waiting = (n, i, ready)
            moved = later
        contract(*waiting)

    @pl.loop(0, count)
    def _(j):
        copy_in(j).wait()
        copy_waves(j).wait()

        @pl.when(j >= 2)
        def _():
            copy_out(j).wait()

        work(j)
        copy_out(j).start()

    for j in range(max(count - 2, 0), count):
        copy_out(j).wait()


def predict(side, edge, weights, stored, waves, off):
    steps = waves.shape[2]
    columns = waves.shape[3] // 2
    group = GROUP
    chunk = min(CHUNK, columns)
    count = columns // chunk
    size = steps * 16 * columns
    return pl.pallas_call(
        functools.partial(predict_kernel, steps, group),
        in_specs=[SM, VM, VM, HB, HB, VM],
        out_specs=[VM, HB],
        out_shape=[
            jax.ShapeDtypeStruct((16, columns), F32),
            jax.ShapeDtypeStruct((steps * 16, columns), F32),
        ],
        scratch_shapes=[
            pltpu.VMEM((steps, 2, columns // 16, LANES), BF),
            pltpu.SemaphoreType.DMA((count,)),
            pltpu.VMEM((2, 2, steps, columns), F32),
            pltpu.SemaphoreType.DMA((count,)),
            pltpu.VMEM((2, steps * 16, chunk), F32),
            pltpu.SemaphoreType.DMA((2,)),
        ],
        compiler_params=pltpu.CompilerParams(vmem_limit_bytes=50 << 20),
        cost_estimate=pl.CostEstimate(flops=200 * size, bytes_accessed=6 * size, transcendentals=0),
        name="predict",
    )(jnp.stack([side, edge]).astype(jnp.int32), permutation(group), weights, stored, waves, off)


def correct_kernel(steps, group, sc_ref, k_ref, turned_ref, start_ref, pred_ref, out_ref, held, sems, wide_ref):
    columns = out_ref.shape[-1]
    chunk = min(CHUNK, columns)
    count = columns // chunk
    width = 2 * LANES
    rows = 16 * group
    base = sc_ref[0] * columns

    def copy_in(j):
        lanes = pl.ds(pl.multiple_of(j * chunk, chunk), chunk)
        return pltpu.make_async_copy(turned_ref.at[:, lanes], held.at[:, lanes], sems.at[j])

    for j in range(count):
        copy_in(j).start()

    def work(j):
        items = [(n, i) for n in range(chunk // width) for i in range(steps // group)]
        sums = {}

        def span(n):
            return pl.ds(pl.multiple_of(j * chunk + n * width, width), width)

        def contract(n, i, top, low):
            first = jnp.dot(k_ref[i], top, preferred_element_type=F32)
            second = jnp.dot(k_ref[i, :16], low, preferred_element_type=F32)
            if i > 0:
                first, second = sums[n][0] + first, sums[n][1] + second
            sums[n] = first, second
            if i == steps // group - 1:
                out_ref[:, span(n)] = (first[:16] + first[16:]) + second

        waiting = None
        for n, i in items:
            if waiting is not None:
                contract(*waiting)
            if i == 0:
                full = start_ref[:, pl.ds(pl.multiple_of(base + j * chunk + n * width, width), width)] + pred_ref[:, span(n)]
                full = 0.25 * full
                for c in range(16):
                    wide_ref[n, c] = jnp.broadcast_to(full[c : c + 1], (8, width))
            parts = []
            for g in range(group // 8):
                at = i * rows + 128 * g
                turned = [held[at + 8 * c : at + 8 * c + 8, span(n)] for c in range(16)]
                terms = [turned[c] * wide_ref[n, c] for c in range(16)]
                while len(terms) > 1:
                    terms = [terms[m] + terms[m + 1] for m in range(0, len(terms), 2)]
                vertex = 1.0 / (1.0 + terms[0] * terms[0])
                parts += [vertex * x for x in turned]
            x = jnp.concatenate(parts, axis=0)
            top = x.astype(BF)
            waiting = (n, i, top, (x - top.astype(F32)).astype(BF))
        contract(*waiting)

    @pl.loop(0, count)
    def _(j):
        copy_in(j).wait()
        work(j)


def correct(side, weights, turned, start, pred):
    columns = pred.shape[1]
    steps = turned.shape[0] // 16
    group = GROUP
    chunk = min(CHUNK, columns)
    size = steps * 16 * columns
    return pl.pallas_call(
        functools.partial(correct_kernel, steps, group),
        in_specs=[SM, VM, HB, VM, VM],
        out_specs=VM,
        out_shape=jax.ShapeDtypeStruct((16, columns), F32),
        scratch_shapes=[
            pltpu.VMEM(turned.shape, F32),
            pltpu.SemaphoreType.DMA((columns // chunk,)),
            pltpu.VMEM((chunk // (2 * LANES), 16, 8, 2 * LANES), F32),
        ],
        compiler_params=pltpu.CompilerParams(vmem_limit_bytes=46 << 20),
        cost_estimate=pl.CostEstimate(flops=120 * size, bytes_accessed=4 * size, transcendentals=0),
        name="correct",
    )(jnp.reshape(side, (1,)).astype(jnp.int32), weights, turned, start, pred)


def carry_kernel(piece, stored_ref, *rest):
    new_ref, held, in_sems, out_sems = rest[-4:]
    steps = stored_ref.shape[0]
    each = held.shape[0]
    count = in_sems.shape[0]
    part = each // count

    def ends(p):
        here = held.at[pl.ds(p * part, part)]
        there = pl.ds(piece * each + p * part, part)
        read = pltpu.make_async_copy(stored_ref.at[there], here, in_sems.at[p])
        write = pltpu.make_async_copy(here, new_ref.at[there], out_sems.at[p])
        return read, write

    both = [ends(p) for p in range(count)]
    for read, _ in both:
        read.start()
    for read, write in both:
        read.wait()
        write.start()
    for _, write in both:
        write.wait()


def carry(piece, stored, new=None):
    steps = stored.shape[0]
    each = steps // pieces_of(steps)
    count = 4 if each % 4 == 0 else 1
    args = [stored] if new is None else [stored, new]
    size = 4 * stored.size // pieces_of(steps)
    return pl.pallas_call(
        functools.partial(carry_kernel, piece),
        in_specs=[HB] * len(args),
        out_specs=HB,
        out_shape=jax.ShapeDtypeStruct(stored.shape, stored.dtype),
        scratch_shapes=[
            pltpu.VMEM((each, *stored.shape[1:]), BF),
            pltpu.SemaphoreType.DMA((count,)),
            pltpu.SemaphoreType.DMA((count,)),
        ],
        input_output_aliases={} if new is None else {1: 0},
        compiler_params=pltpu.CompilerParams(vmem_limit_bytes=46 << 20),
        cost_estimate=pl.CostEstimate(flops=0, bytes_accessed=size, transcendentals=0),
        name="carry",
    )(*args)


def finish_kernel(sc_ref, old_ref, own_ref, other_ref, whole_ref, new_ref, held, sem):
    half = own_ref.shape[1]
    side = sc_ref[0]
    for at, ref in ((side, own_ref), (1 - side, other_ref)):
        whole_ref[:, pl.ds(pl.multiple_of(at * half, LANES), half)] = ref[...]

    @pl.when(sc_ref[1] == 1)
    def _():
        for at, ref in ((side, own_ref), (1 - side, other_ref)):
            for part in range(2):
                for n in range(half // (2 * LANES)):
                    tiles = [
                        ref[8 * part : 8 * part + 8, (2 * n + t) * LANES : (2 * n + t + 1) * LANES] for t in range(2)
                    ]
                    rows = pl.ds(pl.multiple_of(at * (half // 16) + 16 * n, 16), 16)
                    held[part, rows] = jnp.concatenate(tiles, axis=0).astype(BF)
        copy = pltpu.make_async_copy(held, new_ref.at[sc_ref[2]], sem)
        copy.start()
        copy.wait()


def finish(side, own, slot, new, new_own, new_other):
    rows, half = new_own.shape
    return pl.pallas_call(
        finish_kernel,
        in_specs=[SM, HB, VM, VM],
        out_specs=[VM, HB],
        out_shape=[jax.ShapeDtypeStruct((rows, 2 * half), F32), jax.ShapeDtypeStruct(new.shape, new.dtype)],
        scratch_shapes=[pltpu.VMEM(new.shape[1:], BF), pltpu.SemaphoreType.DMA],
        input_output_aliases={1: 1},
        compiler_params=pltpu.CompilerParams(vmem_limit_bytes=40 << 20),
        name="finish",
    )(jnp.stack([side, own, slot]).astype(jnp.int32), new, new_own, new_other)


def tiled(x):
    lead, columns = x.shape[:-2], x.shape[-1]
    x = x.reshape(*lead, 2, 8, columns // LANES, LANES)
    return jnp.swapaxes(x, -3, -2).reshape(*lead, 2, columns // 16, LANES)


def untiled(x):
    lead, rows = x.shape[:-3], x.shape[-2]
    x = jnp.swapaxes(x.reshape(*lead, 2, rows // 8, 8, LANES), -3, -2)
    return x.reshape(*lead, 16, rows * 16)


def rotate(values, angles):
    columns = angles.shape[-1]
    spread = jnp.broadcast_to(angles[None, :, None, :], (2, 2, 2, columns)).reshape(8, columns)
    c, s = jnp.cos(spread), jnp.sin(spread)
    real, imag = values[:8], values[8:]
    return jnp.concatenate([c * real + s * imag, c * imag - s * real], axis=0)


def on_device(history, energy, kernel, newest, current, step_energy):
    steps, _, columns = history.shape
    count = lax.axis_size("ta")
    place_here = lax.axis_index("ta")
    bits = count.bit_length() - 1
    half = columns // 2
    latest = newest[0]
    owner = lax.div(latest, steps)
    edge = latest - place_here * steps
    side = place_here & 1
    other = 1 - side

    def swap(x, mask):
        return lax.ppermute(x, "ta", [(i, i ^ mask) for i in range(count)])

    masks = [2] + [6 if t == 2 else 1 << t for t in range(2, bits)]
    split = (place_here >> 1 ^ place_here >> 2) & 1

    mine = place_here == owner
    value, late = totals(edge, energy)
    waves = trig(energy)

    total, ahead = value, jnp.zeros_like(value)
    for t in range(bits):
        mask = 6 if t == 2 else 1 << t
        got = swap(total, mask)
        here, there = place_here >> t, owner >> t
        upper = (here & 1) == 1
        partner = here ^ 1
        counted_low = ~((there == here) & (place_here < owner))
        counted_high = (there == partner) | ((there == here) & (place_here >= owner))
        ahead = ahead + jnp.where(jnp.where(upper, counted_high, counted_low), got, 0.0)
        low_group = jnp.where(upper, partner, here)
        total = jnp.where(there == low_group, jnp.where(upper, got, total), total + got)
    off = jnp.stack([jnp.where(mine, -late, ahead), jnp.where(mine, ahead + value, ahead)])
    off_sin, off_cos = sincos(off)
    off = jnp.stack([off_cos, off_sin])

    weights = kernel_rows(kernel)
    stored = tiled(history)
    start = rotate(current, step_energy)

    new = None
    piece = 0

    def swap_beside(x, mask):
        nonlocal new, piece
        if piece == pieces_of(steps):
            return swap(x, mask)
        x, here = lax.optimization_barrier((x, stored))
        got = swap(x, mask)
        got, new = lax.optimization_barrier((got, carry(piece, here, new)))
        piece += 1
        return got

    first = split == 0

    def inner_part(x):
        keep = jnp.where(first, x[:8], x[8:])
        send = jnp.where(first, x[8:], x[:8])
        keep = keep + swap_beside(send, masks[0])
        for mask in masks[1:]:
            keep = keep + swap_beside(keep, mask)
        return keep

    def joined(keep, rest):
        return jnp.concatenate([jnp.where(first, keep, rest), jnp.where(first, rest, keep)], axis=0)

    part_other, turned_other = predict(other, edge, weights, stored, waves, off)
    from_partner = swap(part_other, 1)
    part_own, turned_own = predict(side, edge, weights, stored, waves, off)
    pred_own = inner_part(part_own + from_partner)
    pred_own = joined(pred_own, swap_beside(pred_own, masks[0]))
    pred_other = swap(pred_own, 1)
    corr_own = correct(side, weights, turned_own, start, pred_own)
    from_partner = swap(corr_own, 1)
    corr_other = correct(other, weights, turned_other, start, pred_other)
    def mine_of(x):
        x = jnp.where(side == 0, x[:, half:], x[:, :half]) if x.shape[1] > half else x
        return jnp.where(first, x[:8], x[8:])

    corr = inner_part(corr_other + from_partner)
    fresh = mine_of(start) + 0.5 * (mine_of(pred_other) + corr)
    gathered = [swap(fresh, mask) for mask in (masks[0], masks[0] ^ 1, 1)]
    new_other = joined(fresh, gathered[0])
    new_own = joined(gathered[2], gathered[1])
    while piece < pieces_of(steps):
        new = carry(piece, stored, new)
        piece += 1
    target = lax.rem(latest + 1, steps * count)
    own = lax.div(target, steps) == place_here
    corrected, new = finish(side, own, lax.rem(target, steps), new, new_own, new_other)
    return corrected, untiled(new)


def solution(mesh):
    return jax.shard_map(
        on_device,
        mesh=mesh,
        in_specs=(
            P("ta", None, "ka"),
            P("ta", None, "ka"),
            P("ta", None, None),
            P(),
            P(None, "ka"),
            P(None, "ka"),
        ),
        out_specs=(P(None, "ka"), P("ta", None, "ka")),
        check_vma=False,
    )
```

```python
import functools

import jax
import jax.numpy as jnp
import numpy as np
from jax import lax
from jax.experimental import pallas as pl
from jax.experimental.pallas import tpu as pltpu
from jax.sharding import PartitionSpec as P

LANES = 128
WIDE = 4 * LANES
CHUNK = 1024
VM = pl.BlockSpec(memory_space=pltpu.VMEM)
SM = pl.BlockSpec(memory_space=pltpu.SMEM)
HB = pl.BlockSpec(memory_space=pltpu.HBM)
SIN = (1.41420874, -0.235676110, 0.0117467684, -2.59660918e-4)
COS = (1.41421350, -0.707105432, 0.0589211807, -1.95919014e-3, 3.27400865e-5)
BF = jnp.bfloat16
F32 = jnp.float32
SELF = [slice(t * LANES, (t + 1) * LANES) for t in range(4)]


GROUP = 8


def double_sincos(u):
    q = u * u
    z = u * (SIN[0] + q * (SIN[1] + q * (SIN[2] + q * SIN[3])))
    c = COS[0] + q * (COS[1] + q * (COS[2] + q * (COS[3] + q * COS[4])))
    return z * c, 1.0 - z * z


def half_angle_sincos(half):
    return double_sincos(half - jnp.round(half * (1.0 / np.pi)) * np.pi)


def sincos(angle):
    half = 0.5 * angle
    turns = jnp.round(half * (1.0 / np.pi))
    return double_sincos((half - turns * 3.140625) - turns * 9.67653589793e-4)


def pieces_of(steps):
    return 4 if steps % 4 == 0 else 1


def totals_kernel(edge_ref, energy_ref, value_ref, late_ref, held, sems):
    steps = energy_ref.shape[0]
    pieces = pieces_of(steps)
    each = steps // pieces
    edge = edge_ref[0]

    def copy(p):
        part = pl.ds(p * each, each)
        return pltpu.make_async_copy(energy_ref.at[part], held.at[part], sems.at[p])

    for p in range(pieces):
        copy(p).start()
    total = jnp.zeros(value_ref.shape, F32)
    late = jnp.zeros(value_ref.shape, F32)
    for p in range(pieces):
        copy(p).wait()
        for s in range(p * each, (p + 1) * each):
            e = held[s]
            total = total + e
            late = late + e * (s > edge).astype(F32)
    mine = (edge >= 0) & (edge < steps)
    value_ref[...] = jnp.where(mine, total - late, total)
    late_ref[...] = late


def totals(edge, energy):
    steps, _, columns = energy.shape
    rows = columns // (LANES // 2)
    view = energy.reshape(steps, 2, columns // LANES, LANES).transpose(0, 2, 1, 3).reshape(steps, rows, LANES)
    return pl.pallas_call(
        totals_kernel,
        in_specs=[SM, HB],
        out_specs=[VM, VM],
        out_shape=[jax.ShapeDtypeStruct((rows, LANES), F32)] * 2,
        scratch_shapes=[pltpu.VMEM(view.shape, F32), pltpu.SemaphoreType.DMA((pieces_of(steps),))],
        compiler_params=pltpu.CompilerParams(vmem_limit_bytes=51 << 20),
        cost_estimate=pl.CostEstimate(flops=4 * energy.size, bytes_accessed=4 * energy.size, transcendentals=0),
        name="totals",
    )(jnp.reshape(edge, (1,)).astype(jnp.int32), view)


def trig_kernel(side_ref, tri_ref, energy_ref, waves_ref, held, made, in_sems, out_sems):
    columns = held.shape[-1]
    chunk = min(CHUNK, columns)
    count = columns // chunk

    def copy_in(j, a):
        there = pl.ds(pl.multiple_of(side_ref[0] * columns + j * chunk, chunk), chunk)
        lanes = pl.ds(j * chunk, chunk)
        return pltpu.make_async_copy(energy_ref.at[:, a, there], held.at[a, :, lanes], in_sems.at[j, a])

    def copy_out(j):
        lanes = pl.ds(j * chunk, chunk)
        return pltpu.make_async_copy(made.at[:, :, :, lanes], waves_ref.at[:, :, :, lanes], out_sems.at[j])

    for j in range(count):
        for a in range(2):
            copy_in(j, a).start()
    for j in range(count):
        for a in range(2):
            copy_in(j, a).wait()
        for n in range(chunk // WIDE):
            lanes = slice(j * chunk + n * WIDE, j * chunk + (n + 1) * WIDE)
            for a in range(2):
                e = held[a, :, lanes]
                top = e.astype(BF)
                rest = e - top.astype(F32)
                mid = rest.astype(BF)
                low = (rest - mid.astype(F32)).astype(BF)
                half = jnp.dot(
                    tri_ref[...],
                    jnp.concatenate([top, mid, low], axis=0),
                    preferred_element_type=F32,
                )
                s, c = half_angle_sincos(half)
                made[0, a, :, lanes] = c
                made[1, a, :, lanes] = s
        copy_out(j).start()
    for j in range(count):
        copy_out(j).wait()


def trig(side, energy):
    steps, columns = energy.shape[0], energy.shape[2] // 2
    tri = 0.5 * np.triu(np.ones((steps, steps), np.float32))
    tri = jnp.asarray(np.concatenate([tri] * 3, axis=1), BF)
    count = columns // min(CHUNK, columns)
    size = (2, 2, steps, columns)
    return pl.pallas_call(
        trig_kernel,
        in_specs=[SM, VM, HB],
        out_specs=HB,
        out_shape=jax.ShapeDtypeStruct(size, F32),
        scratch_shapes=[
            pltpu.VMEM(size[1:], F32),
            pltpu.VMEM(size, F32),
            pltpu.SemaphoreType.DMA((count, 2)),
            pltpu.SemaphoreType.DMA((count,)),
        ],
        compiler_params=pltpu.CompilerParams(vmem_limit_bytes=54 << 20),
        cost_estimate=pl.CostEstimate(flops=20 * energy.size, bytes_accessed=6 * energy.size, transcendentals=0),
        name="trig",
    )(jnp.reshape(side, (1,)).astype(jnp.int32), tri, energy)


def permutation(group):
    rows = 16 * group
    p = np.zeros((rows, rows), np.float32)
    for tile in range(2):
        for c in range(8):
            for g in range(group // 8):
                for s in range(8):
                    p[((tile * 8 + c) * (group // 8) + g) * 8 + s, ((8 * g + s) * 2 + tile) * 8 + c] = 1
    return jnp.asarray(p, BF)


def kernel_rows(kernel):
    steps = kernel.shape[0]
    group = GROUP
    k = kernel.reshape(steps // group, group // 8, 8, 16, 16).transpose(0, 3, 1, 4, 2)
    k = k.reshape(steps // group, 16, 16 * group)
    top = lax.reduce_precision(k, 8, 7)
    return jnp.concatenate([top, k - top], axis=1).astype(BF)


def predict_kernel(inside, steps, group, sc_ref, perm_ref, k_ref, h_ref, waves_ref, off_ref, out_ref, *rest):
    near_ref, far_ref, held, in_sems, waves, wave_sems, kept, out_sems = rest
    columns = out_ref.shape[-1]
    chunk = kept.shape[-1]
    count = columns // chunk
    tiles = chunk // LANES
    blocks = group // 8
    edge = sc_ref[1]

    def copy_in(j):
        there = pl.ds(pl.multiple_of((sc_ref[0] * (columns // LANES) + j * tiles) * 8, 16), tiles * 8)
        here = pl.ds(pl.multiple_of(j * tiles * 8, 16), tiles * 8)
        return pltpu.make_async_copy(h_ref.at[:, :, there], held.at[:, :, here], in_sems.at[j])

    def copy_out(j, near):
        there = pl.ds(pl.multiple_of((j if near else j - inside) * chunk, chunk), chunk)
        return pltpu.make_async_copy(
            kept.at[j % 2], (near_ref if near else far_ref).at[:, there], out_sems.at[j % 2]
        )

    def copy_waves(j):
        lanes = pl.ds(pl.multiple_of(j * chunk, chunk), chunk)
        return pltpu.make_async_copy(waves_ref.at[:, :, :, lanes], waves.at[:, :, :, lanes], wave_sems.at[j])

    for j in range(count):
        copy_in(j).start()
        copy_waves(j).start()

    def spans(j, n):
        first = j * chunk + n * WIDE
        local = [pl.ds(pl.multiple_of(first + LANES * t, LANES), LANES) for t in range(4)]
        return local

    def pair(part, a, s0, local, t):
        rows = slice(s0, s0 + 8)
        return jnp.concatenate([waves[part, a, rows, local[t]], waves[part, a, rows, local[t + 2]]], axis=-1)

    def off_row(part, later_side, j, n, t, a):
        row = 2 * ((sc_ref[0] * (columns // LANES)) + j * tiles + 4 * n + t) + a
        return jnp.concatenate(
            [off_ref[part, later_side, pl.ds(row, 1)], off_ref[part, later_side, pl.ds(row + 4, 1)]], axis=-1
        )

    def move(j, n, i):
        row = pl.multiple_of(j * tiles * 8 + n * 32, 16)
        moved = []
        for part in range(2):
            h = [
                held[i * group : (i + 1) * group, part, pl.ds(pl.multiple_of(row + 16 * p, 16), 16)].reshape(
                    16 * group, LANES
                )
                for p in range(2)
            ]
            moved.append(jnp.dot(perm_ref[...], jnp.concatenate(h, axis=1), preferred_element_type=F32))
        return moved

    def turned_rows(local, i, t, g, moved, turn):
        s0 = i * group + 8 * g
        after = lax.broadcasted_iota(jnp.int32, (8, 2 * LANES), 0) + s0 > edge
        angle = []
        for a in range(2):
            c = pair(0, a, s0, local, t)
            s = pair(1, a, s0, local, t)
            co = jnp.where(after, turn[t][1][a], turn[t][0][a])
            so = jnp.where(after, turn[2 + t][1][a], turn[2 + t][0][a])
            angle.append((c * co - s * so, s * co + c * so))
        real, imag = [], []
        for e in range(8):
            c, s = angle[(e >> 1) & 1]
            at = ((t * 8 + e) * blocks + g) * 8
            x = moved[0][at : at + 8]
            y = moved[1][at : at + 8]
            real.append(c * x + s * y)
            imag.append(c * y - s * x)
        return real + imag

    def work(j):
        items = [(n, i) for n in range(chunk // WIDE) for i in range(steps // group)]
        sums = {}
        buf = j % 2

        def contract(n, i, ready):
            for t in range(2):
                top, low = ready[t]
                first = jnp.dot(k_ref[i], top, preferred_element_type=F32)
                second = jnp.dot(k_ref[i, :16], low, preferred_element_type=F32)
                if i > 0:
                    first, second = sums[n, t][0] + first, sums[n, t][1] + second
                sums[n, t] = first, second
                if i == steps // group - 1:
                    total = (first[:16] + first[16:]) + second
                    local = spans(j, n)
                    out_ref[:, local[t]] = total[:, :LANES]
                    out_ref[:, local[t + 2]] = total[:, LANES:]

        moved = move(j, *items[0])
        waiting = None
        for at, (n, i) in enumerate(items):
            if waiting is not None:
                contract(*waiting)
            later = move(j, *items[at + 1]) if at + 1 < len(items) else None
            local = spans(j, n)
            if i == 0:
                turn = [
                    [[off_row(part, later_side, j, n, t, a) for a in range(2)] for later_side in range(2)]
                    for part in range(2)
                    for t in range(2)
                ]
            ready = []
            rows = slice(i * 16 * group, (i + 1) * 16 * group)
            for t in range(2):
                x = jnp.concatenate(
                    [row for g in range(blocks) for row in turned_rows(local, i, t, g, moved, turn)], axis=0
                )
                kept[buf, rows, n * WIDE + t * LANES : n * WIDE + (t + 1) * LANES] = x[:, :LANES]
                kept[buf, rows, n * WIDE + (t + 2) * LANES : n * WIDE + (t + 3) * LANES] = x[:, LANES:]
                top = x.astype(BF)
                ready.append((top, (x - top.astype(F32)).astype(BF)))
            waiting = (n, i, ready)
            moved = later
        contract(*waiting)

    def span(first, last, near):
        @pl.loop(first, last)
        def _(j):
            copy_in(j).wait()
            copy_waves(j).wait()

            @pl.when(j >= 2)
            def _():
                copy_out(j, near).wait()

            work(j)
            copy_out(j, near).start()

    span(0, inside, True)
    span(inside, count, False)
    for j in range(max(count - 2, 0), count):
        copy_out(j, j < inside).wait()


def predict(side, edge, weights, stored, waves, off):
    steps = waves.shape[2]
    columns = waves.shape[3]
    group = GROUP
    chunk = min(CHUNK, columns)
    count = columns // chunk
    inside = count // 2
    size = steps * 16 * columns
    return pl.pallas_call(
        functools.partial(predict_kernel, inside, steps, group),
        in_specs=[SM, VM, VM, HB, HB, VM],
        out_specs=[VM, HB, HB],
        out_shape=[jax.ShapeDtypeStruct((16, columns), F32)]
        + [jax.ShapeDtypeStruct((steps * 16, c), F32) for c in (inside * chunk, columns - inside * chunk)],
        scratch_shapes=[
            pltpu.VMEM((steps, 2, columns // 16, LANES), BF),
            pltpu.SemaphoreType.DMA((count,)),
            pltpu.VMEM((2, 2, steps, columns), F32),
            pltpu.SemaphoreType.DMA((count,)),
            pltpu.VMEM((2, steps * 16, chunk), F32),
            pltpu.SemaphoreType.DMA((2,)),
        ],
        compiler_params=pltpu.CompilerParams(vmem_limit_bytes=51 << 20),
        cost_estimate=pl.CostEstimate(flops=200 * size, bytes_accessed=6 * size, transcendentals=0),
        name="predict",
    )(jnp.stack([side, edge]).astype(jnp.int32), permutation(group), weights, stored, waves, off)


def correct_kernel(inside, steps, group, sc_ref, k_ref, start_ref, pred_ref, *rest):
    near_ref = rest[0] if inside else None
    far_ref, out_ref, held, sems, wide_ref = rest[-5:]
    columns = out_ref.shape[-1]
    chunk = min(CHUNK, columns)
    count = columns // chunk
    width = 2 * LANES
    rows = 16 * group
    base = sc_ref[0] * columns

    def copy_in(j):
        lanes = pl.ds(pl.multiple_of(j * chunk, chunk), chunk)
        return pltpu.make_async_copy(far_ref.at[:, lanes], held.at[:, lanes], sems.at[j])

    for j in range(count - inside):
        copy_in(j).start()

    def work(j, source, offset):
        items = [(n, i) for n in range(chunk // width) for i in range(steps // group)]
        sums = {}

        def span(n):
            return pl.ds(pl.multiple_of(j * chunk + n * width, width), width)

        def contract(n, i, top, low):
            first = jnp.dot(k_ref[i], top, preferred_element_type=F32)
            second = jnp.dot(k_ref[i, :16], low, preferred_element_type=F32)
            if i > 0:
                first, second = sums[n][0] + first, sums[n][1] + second
            sums[n] = first, second
            if i == steps // group - 1:
                out_ref[:, span(n)] = (first[:16] + first[16:]) + second

        waiting = None
        for n, i in items:
            if waiting is not None:
                contract(*waiting)
            if i == 0:
                full = start_ref[:, pl.ds(pl.multiple_of(base + j * chunk + n * width, width), width)] + pred_ref[:, span(n)]
                full = 0.25 * full
                for c in range(16):
                    wide_ref[n, c] = jnp.broadcast_to(full[c : c + 1], (8, width))
            parts = []
            here = pl.ds(pl.multiple_of((j - offset) * chunk + n * width, width), width)
            for g in range(group // 8):
                at = i * rows + 128 * g
                turned = [source[at + 8 * c : at + 8 * c + 8, here] for c in range(16)]
                terms = [turned[c] * wide_ref[n, c] for c in range(16)]
                while len(terms) > 1:
                    terms = [terms[m] + terms[m + 1] for m in range(0, len(terms), 2)]
                vertex = 1.0 / (1.0 + terms[0] * terms[0])
                parts += [vertex * x for x in turned]
            x = jnp.concatenate(parts, axis=0)
            top = x.astype(BF)
            waiting = (n, i, top, (x - top.astype(F32)).astype(BF))
        contract(*waiting)

    if inside:

        @pl.loop(0, inside)
        def _(j):
            work(j, near_ref, 0)

    @pl.loop(inside, count)
    def _(j):
        copy_in(j - inside).wait()
        work(j, held, inside)


def correct(side, weights, start, pred, *turned):
    columns = pred.shape[1]
    steps = turned[0].shape[0] // 16
    group = GROUP
    chunk = min(CHUNK, columns)
    size = steps * 16 * columns
    far = turned[-1]
    inside = (columns - far.shape[1]) // chunk
    return pl.pallas_call(
        functools.partial(correct_kernel, inside, steps, group),
        in_specs=[SM, VM, VM, VM] + [VM] * (inside > 0) + [HB],
        out_specs=VM,
        out_shape=jax.ShapeDtypeStruct((16, columns), F32),
        scratch_shapes=[
            pltpu.VMEM(far.shape, F32),
            pltpu.SemaphoreType.DMA((columns // chunk - inside,)),
            pltpu.VMEM((chunk // (2 * LANES), 16, 8, 2 * LANES), F32),
        ],
        compiler_params=pltpu.CompilerParams(vmem_limit_bytes=44 << 20),
        cost_estimate=pl.CostEstimate(flops=120 * size, bytes_accessed=4 * size, transcendentals=0),
        name="correct",
    )(jnp.reshape(side, (1,)).astype(jnp.int32), weights, start, pred, *turned)


def carry_kernel(piece, stored_ref, *rest):
    new_ref, held, in_sems, out_sems = rest[-4:]
    steps = stored_ref.shape[0]
    each = held.shape[0]
    count = in_sems.shape[0]
    part = each // count

    def ends(p):
        here = held.at[pl.ds(p * part, part)]
        there = pl.ds(piece * each + p * part, part)
        read = pltpu.make_async_copy(stored_ref.at[there], here, in_sems.at[p])
        write = pltpu.make_async_copy(here, new_ref.at[there], out_sems.at[p])
        return read, write

    both = [ends(p) for p in range(count)]
    for read, _ in both:
        read.start()
    for read, write in both:
        read.wait()
        write.start()
    for _, write in both:
        write.wait()


def carry(piece, stored, new=None):
    steps = stored.shape[0]
    each = steps // pieces_of(steps)
    count = 4 if each % 4 == 0 else 1
    args = [stored] if new is None else [stored, new]
    size = 4 * stored.size // pieces_of(steps)
    return pl.pallas_call(
        functools.partial(carry_kernel, piece),
        in_specs=[HB] * len(args),
        out_specs=HB,
        out_shape=jax.ShapeDtypeStruct(stored.shape, stored.dtype),
        scratch_shapes=[
            pltpu.VMEM((each, *stored.shape[1:]), BF),
            pltpu.SemaphoreType.DMA((count,)),
            pltpu.SemaphoreType.DMA((count,)),
        ],
        input_output_aliases={} if new is None else {1: 0},
        compiler_params=pltpu.CompilerParams(vmem_limit_bytes=42 << 20),
        cost_estimate=pl.CostEstimate(flops=0, bytes_accessed=size, transcendentals=0),
        name="carry",
    )(*args)


def finish_kernel(sc_ref, old_ref, own_ref, other_ref, whole_ref, new_ref, held, sem, sems):
    half = own_ref.shape[1]
    side = sc_ref[0]
    places = ((side, own_ref), (1 - side, other_ref))
    writes = [
        pltpu.make_async_copy(ref, whole_ref.at[:, pl.ds(pl.multiple_of(at * half, LANES), half)], sems.at[n])
        for n, (at, ref) in enumerate(places)
    ]
    for write in writes:
        write.start()

    @pl.when(sc_ref[1] == 1)
    def _():
        for at, ref in places:
            for part in range(2):
                for n in range(half // (2 * LANES)):
                    tiles = [
                        ref[8 * part : 8 * part + 8, (2 * n + t) * LANES : (2 * n + t + 1) * LANES] for t in range(2)
                    ]
                    rows = pl.ds(pl.multiple_of(at * (half // 16) + 16 * n, 16), 16)
                    held[part, rows] = jnp.concatenate(tiles, axis=0).astype(BF)
        copy = pltpu.make_async_copy(held, new_ref.at[sc_ref[2]], sem)
        copy.start()
        copy.wait()

    for write in writes:
        write.wait()


def finish(side, own, slot, new, new_own, new_other):
    rows, half = new_own.shape
    return pl.pallas_call(
        finish_kernel,
        in_specs=[SM, HB, VM, VM],
        out_specs=[HB, HB],
        out_shape=[jax.ShapeDtypeStruct((rows, 2 * half), F32), jax.ShapeDtypeStruct(new.shape, new.dtype)],
        scratch_shapes=[
            pltpu.VMEM(new.shape[1:], BF),
            pltpu.SemaphoreType.DMA,
            pltpu.SemaphoreType.DMA((2,)),
        ],
        input_output_aliases={1: 1},
        compiler_params=pltpu.CompilerParams(vmem_limit_bytes=40 << 20),
        name="finish",
    )(jnp.stack([side, own, slot]).astype(jnp.int32), new, new_own, new_other)


def tiled(x):
    lead, columns = x.shape[:-2], x.shape[-1]
    x = x.reshape(*lead, 2, 8, columns // LANES, LANES)
    return jnp.swapaxes(x, -3, -2).reshape(*lead, 2, columns // 16, LANES)


def untiled(x):
    lead, rows = x.shape[:-3], x.shape[-2]
    x = jnp.swapaxes(x.reshape(*lead, 2, rows // 8, 8, LANES), -3, -2)
    return x.reshape(*lead, 16, rows * 16)


def rotate(values, angles):
    columns = angles.shape[-1]
    spread = jnp.broadcast_to(angles[None, :, None, :], (2, 2, 2, columns)).reshape(8, columns)
    c, s = jnp.cos(spread), jnp.sin(spread)
    real, imag = values[:8], values[8:]
    return jnp.concatenate([c * real + s * imag, c * imag - s * real], axis=0)


def on_device(history, energy, kernel, newest, current, step_energy):
    steps, _, columns = history.shape
    count = lax.axis_size("ta")
    place_here = lax.axis_index("ta")
    bits = count.bit_length() - 1
    half = columns // 2
    latest = newest[0]
    owner = lax.div(latest, steps)
    edge = latest - place_here * steps
    side = place_here & 1
    other = 1 - side

    def swap(x, mask):
        return lax.ppermute(x, "ta", [(i, i ^ mask) for i in range(count)])

    masks = [2] + [6 if t == 2 else 1 << t for t in range(2, bits)]
    split = (place_here >> 1 ^ place_here >> 2) & 1

    mine = place_here == owner
    value, late = totals(edge, energy)

    total, ahead = value, jnp.zeros_like(value)
    waves = []
    for t in range(bits):
        mask = 6 if t == 2 else 1 << t
        if t < 2:
            total, seen = lax.optimization_barrier((total, energy))
            got, made = lax.optimization_barrier((swap(total, mask), trig((other, side)[t], seen)))
            waves.append(made)
        else:
            got = swap(total, mask)
        here, there = place_here >> t, owner >> t
        upper = (here & 1) == 1
        partner = here ^ 1
        counted_low = ~((there == here) & (place_here < owner))
        counted_high = (there == partner) | ((there == here) & (place_here >= owner))
        ahead = ahead + jnp.where(jnp.where(upper, counted_high, counted_low), got, 0.0)
        low_group = jnp.where(upper, partner, here)
        total = jnp.where(there == low_group, jnp.where(upper, got, total), total + got)
    off = jnp.stack([jnp.where(mine, -late, ahead), jnp.where(mine, ahead + value, ahead)])
    off_sin, off_cos = sincos(off)
    off = jnp.stack([off_cos, off_sin])

    while len(waves) < 2:
        waves.append(trig((other, side)[len(waves)], energy))
    weights = kernel_rows(kernel)
    stored = tiled(history)
    start = rotate(current, step_energy)

    new = None
    piece = 0

    def swap_beside(x, mask):
        nonlocal new, piece
        if piece == pieces_of(steps):
            return swap(x, mask)
        x, here = lax.optimization_barrier((x, stored))
        got = swap(x, mask)
        got, new = lax.optimization_barrier((got, carry(piece, here, new)))
        piece += 1
        return got

    first = split == 0

    def inner_part(x):
        keep = jnp.where(first, x[:8], x[8:])
        send = jnp.where(first, x[8:], x[:8])
        keep = keep + swap_beside(send, masks[0])
        for mask in masks[1:]:
            keep = keep + swap_beside(keep, mask)
        return keep

    def joined(keep, rest):
        return jnp.concatenate([jnp.where(first, keep, rest), jnp.where(first, rest, keep)], axis=0)

    part_other, *turned_other = predict(other, edge, weights, stored, waves[0], off)
    from_partner = swap(part_other, 1)
    part_own, *turned_own = predict(side, edge, weights, stored, waves[1], off)
    pred_own = inner_part(part_own + from_partner)
    pred_own = joined(pred_own, swap_beside(pred_own, masks[0]))
    pred_other = swap(pred_own, 1)
    corr_own = correct(side, weights, start, pred_own, *turned_own)
    from_partner = swap(corr_own, 1)
    corr_other = correct(other, weights, start, pred_other, *turned_other)
    def mine_of(x):
        x = jnp.where(side == 0, x[:, half:], x[:, :half]) if x.shape[1] > half else x
        return jnp.where(first, x[:8], x[8:])

    corr = inner_part(corr_other + from_partner)
    fresh = mine_of(start) + 0.5 * (mine_of(pred_other) + corr)
    gathered = [swap(fresh, mask) for mask in (masks[0], masks[0] ^ 1, 1)]
    new_other = joined(fresh, gathered[0])
    new_own = joined(gathered[2], gathered[1])
    while piece < pieces_of(steps):
        new = carry(piece, stored, new)
        piece += 1
    target = lax.rem(latest + 1, steps * count)
    own = lax.div(target, steps) == place_here
    corrected, new = finish(side, own, lax.rem(target, steps), new, new_own, new_other)
    return corrected, untiled(new)


def solution(mesh):
    return jax.shard_map(
        on_device,
        mesh=mesh,
        in_specs=(
            P("ta", None, "ka"),
            P("ta", None, "ka"),
            P("ta", None, None),
            P(),
            P(None, "ka"),
            P(None, "ka"),
        ),
        out_specs=(P(None, "ka"), P("ta", None, "ka")),
        check_vma=False,
    )
```

```python
import functools

import jax
import jax.numpy as jnp
import numpy as np
from jax import lax
from jax.experimental import pallas as pl
from jax.experimental.pallas import tpu as pltpu
from jax.sharding import PartitionSpec as P

LANES = 128
WIDE = 4 * LANES
CHUNK = 1024
VM = pl.BlockSpec(memory_space=pltpu.VMEM)
SM = pl.BlockSpec(memory_space=pltpu.SMEM)
HB = pl.BlockSpec(memory_space=pltpu.HBM)
SIN = (1.41420874, -0.235676110, 0.0117467684, -2.59660918e-4)
COS = (1.41421350, -0.707105432, 0.0589211807, -1.95919014e-3, 3.27400865e-5)
BF = jnp.bfloat16
F32 = jnp.float32
SELF = [slice(t * LANES, (t + 1) * LANES) for t in range(4)]


GROUP = 8


def double_sincos(u):
    q = u * u
    z = u * (SIN[0] + q * (SIN[1] + q * (SIN[2] + q * SIN[3])))
    c = COS[0] + q * (COS[1] + q * (COS[2] + q * (COS[3] + q * COS[4])))
    return z * c, 1.0 - z * z


def half_sincos(half):
    turns = jnp.round(half * (1.0 / np.pi))
    return double_sincos((half - turns * 3.140625) - turns * 9.67653589793e-4)


def pieces_of(steps):
    return 4 if steps % 4 == 0 else 1


def totals_kernel(edge_ref, energy_ref, value_ref, late_ref, held, sems):
    steps = energy_ref.shape[0]
    pieces = pieces_of(steps)
    each = steps // pieces
    edge = edge_ref[0]

    def copy(p):
        part = pl.ds(p * each, each)
        return pltpu.make_async_copy(energy_ref.at[part], held.at[part], sems.at[p])

    for p in range(pieces):
        copy(p).start()
    total = jnp.zeros(value_ref.shape, F32)
    late = jnp.zeros(value_ref.shape, F32)
    for p in range(pieces):
        copy(p).wait()
        for s in range(p * each, (p + 1) * each):
            e = held[s]
            total = total + e
            late = late + e * (s > edge).astype(F32)
    mine = (edge >= 0) & (edge < steps)
    value_ref[...] = jnp.where(mine, total - late, total)
    late_ref[...] = late


def totals(edge, energy):
    steps, _, columns = energy.shape
    rows = columns // (LANES // 2)
    view = energy.reshape(steps, 2, columns // LANES, LANES).transpose(0, 2, 1, 3).reshape(steps, rows, LANES)
    return pl.pallas_call(
        totals_kernel,
        in_specs=[SM, HB],
        out_specs=[VM, VM],
        out_shape=[jax.ShapeDtypeStruct((rows, LANES), F32)] * 2,
        scratch_shapes=[pltpu.VMEM(view.shape, F32), pltpu.SemaphoreType.DMA((pieces_of(steps),))],
        compiler_params=pltpu.CompilerParams(vmem_limit_bytes=51 << 20),
        cost_estimate=pl.CostEstimate(flops=4 * energy.size, bytes_accessed=4 * energy.size, transcendentals=0),
        name="totals",
    )(jnp.reshape(edge, (1,)).astype(jnp.int32), view)


def suffix_rows(steps):
    row = lax.broadcasted_iota(jnp.int32, (steps, 3 * steps), 0)
    column = lax.rem(lax.broadcasted_iota(jnp.int32, (steps, 3 * steps), 1), steps)
    return jnp.where(column >= row, 0.5, 0.0).astype(BF)


def permutation():
    rows = 16 * GROUP
    row = lax.broadcasted_iota(jnp.int32, (rows, rows), 0)
    column = lax.broadcasted_iota(jnp.int32, (rows, rows), 1)
    return jnp.where(column == (row & (GROUP - 1)) * 16 + lax.div(row, GROUP), 1.0, 0.0).astype(BF)


def kernel_rows(kernel):
    steps = kernel.shape[0]
    group = GROUP
    k = kernel.reshape(steps // group, group // 8, 8, 16, 16).transpose(0, 3, 1, 4, 2)
    k = k.reshape(steps // group, 16, 16 * group)
    top = lax.reduce_precision(k, 8, 7)
    return jnp.concatenate([top, k - top], axis=1).astype(BF)


def predict_kernel(inside, steps, group, sc_ref, k_ref, h_ref, energy_ref, off_ref, out_ref, *rest):
    near_ref, far_ref, held, in_sems, energies, energy_sems, halves, waves, kept, out_sems, perm_ref, tri_ref = rest
    columns = out_ref.shape[-1]
    chunk = kept.shape[-1]
    count = columns // chunk
    tiles = chunk // LANES
    blocks = group // 8
    edge = sc_ref[1]

    def copy_in(j):
        there = pl.ds(pl.multiple_of((sc_ref[0] * (columns // LANES) + j * tiles) * 8, 16), tiles * 8)
        here = pl.ds(pl.multiple_of(j * tiles * 8, 16), tiles * 8)
        return pltpu.make_async_copy(h_ref.at[:, :, there], held.at[:, :, here], in_sems.at[j])

    def copy_out(j, near):
        there = pl.ds(pl.multiple_of((j if near else j - inside) * chunk, chunk), chunk)
        return pltpu.make_async_copy(
            kept.at[j % 2], (near_ref if near else far_ref).at[:, there], out_sems.at[j % 2]
        )

    def copy_energy(j, a):
        there = pl.ds(pl.multiple_of(sc_ref[0] * columns + j * chunk, chunk), chunk)
        here = pl.ds(pl.multiple_of(j * chunk, chunk), chunk)
        return pltpu.make_async_copy(energy_ref.at[:, a, there], energies.at[a, :, here], energy_sems.at[j, a])

    def copy_out(j, near):
        there = pl.ds(pl.multiple_of((j if near else j - inside) * chunk, chunk), chunk)
        return pltpu.make_async_copy(
            kept.at[j % 2], (near_ref if near else far_ref).at[:, there], out_sems.at[j % 2]
        )

    def copy_waves(j):
        lanes = pl.ds(pl.multiple_of(j * chunk, chunk), chunk)
        return pltpu.make_async_copy(waves_ref.at[:, :, :, lanes], waves.at[:, :, :, lanes], wave_sems.at[j])

    for j in range(count):
        for a in range(2):
            copy_energy(j, a).start()
        copy_in(j).start()

    def spans(j, n):
        first = j * chunk + n * WIDE
        local = [pl.ds(pl.multiple_of(first + LANES * t, LANES), LANES) for t in range(4)]
        return local

    def pair(n, part, a, s0, t):
        both = [waves[n % 2, part, a, s0 : s0 + 8, LANES * m : LANES * (m + 1)] for m in (t, t + 2)]
        return jnp.concatenate(both, axis=-1)

    def sum_phases(first):
        for a in range(2):
            e = energies[a, :, pl.ds(pl.multiple_of(first, WIDE), WIDE)]
            top = e.astype(BF)
            rest = e - top.astype(F32)
            mid = rest.astype(BF)
            low = (rest - mid.astype(F32)).astype(BF)
            parts = jnp.concatenate([top, mid, low], axis=0)
            halves[a] = jnp.dot(tri_ref[...], parts, preferred_element_type=F32)

    def make_waves(first, n, i):
        after = lax.broadcasted_iota(jnp.int32, (group, WIDE), 0) + i * group > edge
        tile = sc_ref[0] * (columns // LANES) + lax.div(first, LANES)
        rows = slice(i * group, (i + 1) * group)
        for a in range(2):
            low, up = [
                jnp.concatenate([off_ref[later, pl.ds(2 * (tile + t) + a, 1)] for t in range(4)], axis=-1)
                for later in range(2)
            ]
            s, c = half_sincos(halves[a, rows] + jnp.where(after, up, low))
            waves[n % 2, 0, a, rows] = c
            waves[n % 2, 1, a, rows] = s

    def move(j, n, i):
        row = pl.multiple_of(j * tiles * 8 + n * 32, 16)
        moved = []
        for part in range(2):
            h = [
                held[i * group : (i + 1) * group, part, pl.ds(pl.multiple_of(row + 16 * p, 16), 16)].reshape(
                    16 * group, LANES
                )
                for p in range(2)
            ]
            moved.append(jnp.dot(perm_ref[...], jnp.concatenate(h, axis=1), preferred_element_type=F32))
        return moved

    def turned_rows(n, i, t, g, moved):
        s0 = i * group + 8 * g
        angle = [[pair(n, part, a, s0, t) for part in range(2)] for a in range(2)]
        real, imag = [], []
        for e in range(8):
            c, s = angle[(e >> 1) & 1]
            at = ((t * 8 + e) * blocks + g) * 8
            x = moved[0][at : at + 8]
            y = moved[1][at : at + 8]
            real.append(c * x + s * y)
            imag.append(c * y - s * x)
        return real + imag

    def work(j):
        items = [(n, i) for n in range(chunk // WIDE) for i in range(steps // group)]
        sums = {}
        buf = j % 2

        def contract(n, i, ready):
            for t in range(2):
                top, low = ready[t]
                first = jnp.dot(k_ref[i], top, preferred_element_type=F32)
                second = jnp.dot(k_ref[i, :16], low, preferred_element_type=F32)
                if i > 0:
                    first, second = sums[n, t][0] + first, sums[n, t][1] + second
                sums[n, t] = first, second
                if i == steps // group - 1:
                    total = (first[:16] + first[16:]) + second
                    local = spans(j, n)
                    out_ref[:, local[t]] = total[:, :LANES]
                    out_ref[:, local[t + 2]] = total[:, LANES:]

        moved = move(j, *items[0])
        waiting = None
        for at, (n, i) in enumerate(items):
            later = move(j, *items[at + 1]) if at + 1 < len(items) else None
            if waiting is not None:
                contract(*waiting)
            following = jnp.minimum(j * chunk + (n + 1) * WIDE, columns - WIDE)
            if i == 0:
                sum_phases(following)
            make_waves(following, n + 1, i)
            ready = []
            rows = slice(i * 16 * group, (i + 1) * 16 * group)
            for t in range(2):
                x = jnp.concatenate(
                    [row for g in range(blocks) for row in turned_rows(n, i, t, g, moved)], axis=0
                )
                kept[buf, rows, n * WIDE + t * LANES : n * WIDE + (t + 1) * LANES] = x[:, :LANES]
                kept[buf, rows, n * WIDE + (t + 2) * LANES : n * WIDE + (t + 3) * LANES] = x[:, LANES:]
                top = x.astype(BF)
                ready.append((top, (x - top.astype(F32)).astype(BF)))
            waiting = (n, i, ready)
            moved = later
        contract(*waiting)

    def span(first, last, near):
        @pl.loop(first, last)
        def _(j):
            copy_in(j).wait()

            @pl.when(j + 1 < count)
            def _():
                for a in range(2):
                    copy_energy(j + 1, a).wait()

            @pl.when(j >= 2)
            def _():
                copy_out(j, near).wait()

            work(j)
            copy_out(j, near).start()

    perm_ref[...] = permutation()
    tri_ref[...] = suffix_rows(steps)
    for a in range(2):
        copy_energy(0, a).wait()
    sum_phases(0)
    for i in range(steps // group):
        make_waves(0, 0, i)
    span(0, inside, True)
    span(inside, count, False)
    for j in range(max(count - 2, 0), count):
        copy_out(j, j < inside).wait()


def predict(side, edge, weights, stored, energy, off):
    steps, columns = energy.shape[0], energy.shape[2] // 2
    group = GROUP
    chunk = min(CHUNK, columns)
    count = columns // chunk
    inside = count // 2
    size = steps * 16 * columns
    return pl.pallas_call(
        functools.partial(predict_kernel, inside, steps, group),
        in_specs=[SM, VM, HB, HB, VM],
        out_specs=[VM, HB, HB],
        out_shape=[jax.ShapeDtypeStruct((16, columns), F32)]
        + [jax.ShapeDtypeStruct((steps * 16, c), F32) for c in (inside * chunk, columns - inside * chunk)],
        scratch_shapes=[
            pltpu.VMEM((steps, 2, columns // 16, LANES), BF),
            pltpu.SemaphoreType.DMA((count,)),
            pltpu.VMEM((2, steps, columns), F32),
            pltpu.SemaphoreType.DMA((count, 2)),
            pltpu.VMEM((2, steps, WIDE), F32),
            pltpu.VMEM((2, 2, 2, steps, WIDE), F32),
            pltpu.VMEM((2, steps * 16, chunk), F32),
            pltpu.SemaphoreType.DMA((2,)),
            pltpu.VMEM((16 * group, 16 * group), BF),
            pltpu.VMEM((steps, 3 * steps), BF),
        ],
        compiler_params=pltpu.CompilerParams(vmem_limit_bytes=51 << 20),
        cost_estimate=pl.CostEstimate(flops=200 * size, bytes_accessed=6 * size, transcendentals=0),
        name="predict",
    )(
        jnp.stack([side, edge]).astype(jnp.int32),
        weights,
        stored,
        energy,
        off,
    )


def correct_kernel(inside, steps, group, sc_ref, k_ref, start_ref, pred_ref, *rest):
    near_ref = rest[0] if inside else None
    far_ref, out_ref, held, sems, wide_ref = rest[-5:]
    columns = out_ref.shape[-1]
    chunk = min(CHUNK, columns)
    count = columns // chunk
    width = 2 * LANES
    rows = 16 * group
    base = sc_ref[0] * columns

    def copy_in(j):
        lanes = pl.ds(pl.multiple_of(j * chunk, chunk), chunk)
        return pltpu.make_async_copy(far_ref.at[:, lanes], held.at[:, lanes], sems.at[j])

    for j in range(count - inside):
        copy_in(j).start()

    def work(j, source, offset):
        items = [(n, i) for n in range(chunk // width) for i in range(steps // group)]
        sums = {}

        def span(n):
            return pl.ds(pl.multiple_of(j * chunk + n * width, width), width)

        def contract(n, i, top, low):
            first = jnp.dot(k_ref[i], top, preferred_element_type=F32)
            second = jnp.dot(k_ref[i, :16], low, preferred_element_type=F32)
            if i > 0:
                first, second = sums[n][0] + first, sums[n][1] + second
            sums[n] = first, second
            if i == steps // group - 1:
                out_ref[:, span(n)] = (first[:16] + first[16:]) + second

        waiting = None
        for n, i in items:
            if waiting is not None:
                contract(*waiting)
            if i == 0:
                full = start_ref[:, pl.ds(pl.multiple_of(base + j * chunk + n * width, width), width)] + pred_ref[:, span(n)]
                full = 0.25 * full
                for c in range(16):
                    wide_ref[n, c] = jnp.broadcast_to(full[c : c + 1], (8, width))
            parts = []
            here = pl.ds(pl.multiple_of((j - offset) * chunk + n * width, width), width)
            for g in range(group // 8):
                at = i * rows + 128 * g
                turned = [source[at + 8 * c : at + 8 * c + 8, here] for c in range(16)]
                terms = [turned[c] * wide_ref[n, c] for c in range(16)]
                while len(terms) > 1:
                    terms = [terms[m] + terms[m + 1] for m in range(0, len(terms), 2)]
                vertex = 1.0 / (1.0 + terms[0] * terms[0])
                parts += [vertex * x for x in turned]
            x = jnp.concatenate(parts, axis=0)
            top = x.astype(BF)
            waiting = (n, i, top, (x - top.astype(F32)).astype(BF))
        contract(*waiting)

    if inside:

        @pl.loop(0, inside)
        def _(j):
            work(j, near_ref, 0)

    @pl.loop(inside, count)
    def _(j):
        copy_in(j - inside).wait()
        work(j, held, inside)


def correct(side, weights, start, pred, *turned):
    columns = pred.shape[1]
    steps = turned[0].shape[0] // 16
    group = GROUP
    chunk = min(CHUNK, columns)
    size = steps * 16 * columns
    far = turned[-1]
    inside = (columns - far.shape[1]) // chunk
    return pl.pallas_call(
        functools.partial(correct_kernel, inside, steps, group),
        in_specs=[SM, VM, VM, VM] + [VM] * (inside > 0) + [HB],
        out_specs=VM,
        out_shape=jax.ShapeDtypeStruct((16, columns), F32),
        scratch_shapes=[
            pltpu.VMEM(far.shape, F32),
            pltpu.SemaphoreType.DMA((columns // chunk - inside,)),
            pltpu.VMEM((chunk // (2 * LANES), 16, 8, 2 * LANES), F32),
        ],
        compiler_params=pltpu.CompilerParams(vmem_limit_bytes=44 << 20),
        cost_estimate=pl.CostEstimate(flops=120 * size, bytes_accessed=4 * size, transcendentals=0),
        name="correct",
    )(jnp.reshape(side, (1,)).astype(jnp.int32), weights, start, pred, *turned)


def carry_kernel(piece, stored_ref, *rest):
    new_ref, held, in_sems, out_sems = rest[-4:]
    steps = stored_ref.shape[0]
    each = held.shape[0]
    count = in_sems.shape[0]
    part = each // count

    def ends(p):
        here = held.at[pl.ds(p * part, part)]
        there = pl.ds(piece * each + p * part, part)
        read = pltpu.make_async_copy(stored_ref.at[there], here, in_sems.at[p])
        write = pltpu.make_async_copy(here, new_ref.at[there], out_sems.at[p])
        return read, write

    both = [ends(p) for p in range(count)]
    for read, _ in both:
        read.start()
    for read, write in both:
        read.wait()
        write.start()
    for _, write in both:
        write.wait()


def carry(piece, stored, new=None):
    steps = stored.shape[0]
    each = steps // pieces_of(steps)
    count = 4 if each % 4 == 0 else 1
    args = [stored] if new is None else [stored, new]
    size = 4 * stored.size // pieces_of(steps)
    return pl.pallas_call(
        functools.partial(carry_kernel, piece),
        in_specs=[HB] * len(args),
        out_specs=HB,
        out_shape=jax.ShapeDtypeStruct(stored.shape, stored.dtype),
        scratch_shapes=[
            pltpu.VMEM((each, *stored.shape[1:]), BF),
            pltpu.SemaphoreType.DMA((count,)),
            pltpu.SemaphoreType.DMA((count,)),
        ],
        input_output_aliases={} if new is None else {1: 0},
        compiler_params=pltpu.CompilerParams(vmem_limit_bytes=42 << 20),
        cost_estimate=pl.CostEstimate(flops=0, bytes_accessed=size, transcendentals=0),
        name="carry",
    )(*args)


def finish_kernel(sc_ref, old_ref, own_ref, other_ref, whole_ref, new_ref, held, sem, sems):
    half = own_ref.shape[1]
    side = sc_ref[0]
    places = ((side, own_ref), (1 - side, other_ref))
    writes = [
        pltpu.make_async_copy(ref, whole_ref.at[:, pl.ds(pl.multiple_of(at * half, LANES), half)], sems.at[n])
        for n, (at, ref) in enumerate(places)
    ]
    for write in writes:
        write.start()

    @pl.when(sc_ref[1] == 1)
    def _():
        for at, ref in places:
            for part in range(2):
                for n in range(half // (2 * LANES)):
                    tiles = [
                        ref[8 * part : 8 * part + 8, (2 * n + t) * LANES : (2 * n + t + 1) * LANES] for t in range(2)
                    ]
                    rows = pl.ds(pl.multiple_of(at * (half // 16) + 16 * n, 16), 16)
                    held[part, rows] = jnp.concatenate(tiles, axis=0).astype(BF)
        copy = pltpu.make_async_copy(held, new_ref.at[sc_ref[2]], sem)
        copy.start()
        copy.wait()

    for write in writes:
        write.wait()


def finish(side, own, slot, new, new_own, new_other):
    rows, half = new_own.shape
    return pl.pallas_call(
        finish_kernel,
        in_specs=[SM, HB, VM, VM],
        out_specs=[HB, HB],
        out_shape=[jax.ShapeDtypeStruct((rows, 2 * half), F32), jax.ShapeDtypeStruct(new.shape, new.dtype)],
        scratch_shapes=[
            pltpu.VMEM(new.shape[1:], BF),
            pltpu.SemaphoreType.DMA,
            pltpu.SemaphoreType.DMA((2,)),
        ],
        input_output_aliases={1: 1},
        compiler_params=pltpu.CompilerParams(vmem_limit_bytes=40 << 20),
        name="finish",
    )(jnp.stack([side, own, slot]).astype(jnp.int32), new, new_own, new_other)


def tiled(x):
    lead, columns = x.shape[:-2], x.shape[-1]
    x = x.reshape(*lead, 2, 8, columns // LANES, LANES)
    return jnp.swapaxes(x, -3, -2).reshape(*lead, 2, columns // 16, LANES)


def untiled(x):
    lead, rows = x.shape[:-3], x.shape[-2]
    x = jnp.swapaxes(x.reshape(*lead, 2, rows // 8, 8, LANES), -3, -2)
    return x.reshape(*lead, 16, rows * 16)


def rotate(values, angles):
    columns = angles.shape[-1]
    waves = half_sincos(0.5 * angles)
    s, c = [jnp.broadcast_to(x[None, :, None, :], (2, 2, 2, columns)).reshape(8, columns) for x in waves]
    real, imag = values[:8], values[8:]
    return jnp.concatenate([c * real + s * imag, c * imag - s * real], axis=0)


def on_device(history, energy, kernel, newest, current, step_energy):
    steps, _, columns = history.shape
    count = lax.axis_size("ta")
    place_here = lax.axis_index("ta")
    bits = count.bit_length() - 1
    half = columns // 2
    latest = newest[0]
    owner = lax.div(latest, steps)
    edge = latest - place_here * steps
    side = place_here & 1
    other = 1 - side

    def swap(x, mask):
        return lax.ppermute(x, "ta", [(i, i ^ mask) for i in range(count)])

    masks = [2] + [6 if t == 2 else 1 << t for t in range(2, bits)]
    split = (place_here >> 1 ^ place_here >> 2) & 1

    mine = place_here == owner
    value, late = totals(edge, energy)

    total, ahead = value, jnp.zeros_like(value)

    stored = tiled(history)
    new = None
    piece = 0

    def swaps_beside(sent, masks_):
        nonlocal new, piece
        if piece == pieces_of(steps):
            return [swap(x, mask) for x, mask in zip(sent, masks_)]
        sent, here = lax.optimization_barrier((sent, stored))
        got = [swap(x, mask) for x, mask in zip(sent, masks_)]
        got, new = lax.optimization_barrier((got, carry(piece, here, new)))
        piece += 1
        return got

    def counted(t, partner):
        here, there = place_here >> t, owner >> t
        beyond, within = partner > here, partner <= there
        between = jnp.where(here < there, beyond & within, beyond | within)
        return jnp.where(here == there, place_here >= owner, between)

    direct = bits == 3
    for t in range(1 if direct else bits):
        here, there = place_here >> t, owner >> t
        upper, partner = (here & 1) == 1, here ^ 1
        got = swap(total, 6 if t == 2 else 1 << t)
        ahead = ahead + jnp.where(counted(t, partner), got, 0.0)
        low_group = jnp.where(upper, partner, here)
        total = jnp.where(there == low_group, jnp.where(upper, got, total), total + got)
    if direct:
        for mask, got in zip((2, 4, 6), swaps_beside([total] * 3, (2, 4, 6))):
            ahead = ahead + jnp.where(counted(1, (place_here ^ mask) >> 1), got, 0.0)
    start = rotate(current, step_energy)
    off = 0.5 * jnp.stack([jnp.where(mine, -late, ahead), jnp.where(mine, ahead + value, ahead)])
    weights = kernel_rows(kernel)

    first = split == 0

    def inner_part(x, carried):
        keep = jnp.where(first, x[:8], x[8:])
        send = jnp.where(first, x[8:], x[:8])
        for n, mask in enumerate(masks):
            sent = keep if n else send
            (got,) = swaps_beside([sent], [mask]) if carried[min(n, 1)] else [swap(sent, mask)]
            keep = keep + got
        return keep

    def joined(keep, rest):
        return jnp.concatenate([jnp.where(first, keep, rest), jnp.where(first, rest, keep)], axis=0)

    part_other, *turned_other = predict(other, edge, weights, stored, energy, off)
    from_partner = swap(part_other, 1)
    part_own, *turned_own = predict(side, edge, weights, stored, energy, off)
    pred_own = inner_part(part_own + from_partner, (False, True))
    pred_own = joined(pred_own, swap(pred_own, masks[0]))
    pred_other = swap(pred_own, 1)
    corr_own = correct(side, weights, start, pred_own, *turned_own)
    from_partner = swap(corr_own, 1)
    corr_other = correct(other, weights, start, pred_other, *turned_other)
    def mine_of(x):
        x = jnp.where(side == 0, x[:, half:], x[:, :half]) if x.shape[1] > half else x
        return jnp.where(first, x[:8], x[8:])

    corr = inner_part(corr_other + from_partner, (True, True))
    fresh = mine_of(start) + 0.5 * (mine_of(pred_other) + corr)
    gathered = [swap(fresh, mask) for mask in (masks[0], masks[0] ^ 1, 1)]
    new_other = joined(fresh, gathered[0])
    new_own = joined(gathered[2], gathered[1])
    while piece < pieces_of(steps):
        new = carry(piece, stored, new)
        piece += 1
    target = lax.rem(latest + 1, steps * count)
    own = lax.div(target, steps) == place_here
    corrected, new = finish(side, own, lax.rem(target, steps), new, new_own, new_other)
    return corrected, untiled(new)


def solution(mesh):
    return jax.shard_map(
        on_device,
        mesh=mesh,
        in_specs=(
            P("ta", None, "ka"),
            P("ta", None, "ka"),
            P("ta", None, None),
            P(),
            P(None, "ka"),
            P(None, "ka"),
        ),
        out_specs=(P(None, "ka"), P("ta", None, "ka")),
        check_vma=False,
    )
```

```python
import functools

import jax
import jax.numpy as jnp
import numpy as np
from jax import lax
from jax.experimental import pallas as pl
from jax.experimental.pallas import tpu as pltpu
from jax.sharding import PartitionSpec as P

LANES = 128
WIDE = 4 * LANES
CHUNK = 1024
VM = pl.BlockSpec(memory_space=pltpu.VMEM)
SM = pl.BlockSpec(memory_space=pltpu.SMEM)
HB = pl.BlockSpec(memory_space=pltpu.HBM)
SIN = (1.41420874, -0.235676110, 0.0117467684, -2.59660918e-4)
COS = (1.41421350, -0.707105432, 0.0589211807, -1.95919014e-3, 3.27400865e-5)
BF = jnp.bfloat16
F32 = jnp.float32
SELF = [slice(t * LANES, (t + 1) * LANES) for t in range(4)]


GROUP = 8


def double_sincos(u):
    q = u * u
    z = u * (SIN[0] + q * (SIN[1] + q * (SIN[2] + q * SIN[3])))
    c = COS[0] + q * (COS[1] + q * (COS[2] + q * (COS[3] + q * COS[4])))
    return z * c, 1.0 - z * z


def half_sincos(half):
    turns = jnp.round(half * (1.0 / np.pi))
    return double_sincos((half - turns * 3.140625) - turns * 9.67653589793e-4)


def pieces_of(steps):
    return 4 if steps % 4 == 0 else 1


def totals_kernel(edge_ref, energy_ref, value_ref, late_ref, held, sems):
    steps = energy_ref.shape[0]
    pieces = pieces_of(steps)
    each = steps // pieces
    edge = edge_ref[0]

    def copy(p):
        part = pl.ds(p * each, each)
        return pltpu.make_async_copy(energy_ref.at[part], held.at[part], sems.at[p])

    for p in range(pieces):
        copy(p).start()
    total = jnp.zeros(value_ref.shape, F32)
    late = jnp.zeros(value_ref.shape, F32)
    for p in range(pieces):
        copy(p).wait()
        for s in range(p * each, (p + 1) * each):
            e = held[s]
            total = total + e
            late = late + e * (s > edge).astype(F32)
    mine = (edge >= 0) & (edge < steps)
    value_ref[...] = jnp.where(mine, total - late, total)
    late_ref[...] = late


def totals(edge, energy):
    steps, _, columns = energy.shape
    rows = columns // (LANES // 2)
    view = energy.reshape(steps, 2, columns // LANES, LANES).transpose(0, 2, 1, 3).reshape(steps, rows, LANES)
    return pl.pallas_call(
        totals_kernel,
        in_specs=[SM, HB],
        out_specs=[VM, VM],
        out_shape=[jax.ShapeDtypeStruct((rows, LANES), F32)] * 2,
        scratch_shapes=[pltpu.VMEM(view.shape, F32), pltpu.SemaphoreType.DMA((pieces_of(steps),))],
        compiler_params=pltpu.CompilerParams(vmem_limit_bytes=51 << 20),
        cost_estimate=pl.CostEstimate(flops=4 * energy.size, bytes_accessed=4 * energy.size, transcendentals=0),
        name="totals",
    )(jnp.reshape(edge, (1,)).astype(jnp.int32), view)


def suffix_rows(steps):
    row = lax.broadcasted_iota(jnp.int32, (steps, 3 * steps), 0)
    column = lax.rem(lax.broadcasted_iota(jnp.int32, (steps, 3 * steps), 1), steps)
    return jnp.where(column >= row, 0.5, 0.0).astype(BF)


def permutation():
    rows = 16 * GROUP
    row = lax.broadcasted_iota(jnp.int32, (rows, rows), 0)
    column = lax.broadcasted_iota(jnp.int32, (rows, rows), 1)
    return jnp.where(column == (row & (GROUP - 1)) * 16 + lax.div(row, GROUP), 1.0, 0.0).astype(BF)


def kernel_rows(kernel):
    steps = kernel.shape[0]
    group = GROUP
    k = kernel.reshape(steps // group, group // 8, 8, 16, 16).transpose(0, 3, 1, 4, 2)
    k = k.reshape(steps // group, 16, 16 * group)
    top = lax.reduce_precision(k, 8, 7)
    return jnp.concatenate([top, k - top], axis=1).astype(BF)


def predict_kernel(inside, steps, group, sc_ref, k_ref, h_ref, energy_ref, off_ref, out_ref, *rest):
    near_ref, far_ref, held, in_sems, energies, energy_sems, halves, waves, kept, out_sems, perm_ref, tri_ref = rest
    columns = out_ref.shape[-1]
    chunk = kept.shape[-1]
    count = columns // chunk
    tiles = chunk // LANES
    blocks = group // 8
    edge = sc_ref[1]

    def copy_in(j):
        there = pl.ds(pl.multiple_of((sc_ref[0] * (columns // LANES) + j * tiles) * 8, 16), tiles * 8)
        here = pl.ds(pl.multiple_of(j * tiles * 8, 16), tiles * 8)
        return pltpu.make_async_copy(h_ref.at[:, :, there], held.at[:, :, here], in_sems.at[j])

    def copy_out(j, n, near):
        there = pl.ds(pl.multiple_of((j if near else j - inside) * chunk + n * WIDE, WIDE), WIDE)
        here = kept.at[j % 2, :, pl.ds(n * WIDE, WIDE)]
        return pltpu.make_async_copy(here, (near_ref if near else far_ref).at[:, there], out_sems.at[j % 2, n])

    def copy_energy(j, a):
        there = pl.ds(pl.multiple_of(sc_ref[0] * columns + j * chunk, chunk), chunk)
        here = pl.ds(pl.multiple_of(j * chunk, chunk), chunk)
        return pltpu.make_async_copy(energy_ref.at[:, a, there], energies.at[a, :, here], energy_sems.at[j, a])

    for j in range(count):
        for a in range(2):
            copy_energy(j, a).start()
        copy_in(j).start()

    def spans(j, n):
        first = j * chunk + n * WIDE
        local = [pl.ds(pl.multiple_of(first + LANES * t, LANES), LANES) for t in range(4)]
        return local

    def pair(n, part, a, s0, t):
        both = [waves[n % 2, part, a, s0 : s0 + 8, LANES * m : LANES * (m + 1)] for m in (t, t + 2)]
        return jnp.concatenate(both, axis=-1)

    def sum_phases(first):
        for a in range(2):
            e = energies[a, :, pl.ds(pl.multiple_of(first, WIDE), WIDE)]
            top = e.astype(BF)
            rest = e - top.astype(F32)
            mid = rest.astype(BF)
            low = (rest - mid.astype(F32)).astype(BF)
            parts = jnp.concatenate([top, mid, low], axis=0)
            halves[a] = jnp.dot(tri_ref[...], parts, preferred_element_type=F32)

    def make_waves(first, n, i):
        after = lax.broadcasted_iota(jnp.int32, (group, WIDE), 0) + i * group > edge
        tile = sc_ref[0] * (columns // LANES) + lax.div(first, LANES)
        rows = slice(i * group, (i + 1) * group)
        for a in range(2):
            low, up = [
                jnp.concatenate([off_ref[later, pl.ds(2 * (tile + t) + a, 1)] for t in range(4)], axis=-1)
                for later in range(2)
            ]
            s, c = half_sincos(halves[a, rows] + jnp.where(after, up, low))
            waves[n % 2, 0, a, rows] = c
            waves[n % 2, 1, a, rows] = s

    def move(j, n, i):
        row = pl.multiple_of(j * tiles * 8 + n * 32, 16)
        moved = []
        for part in range(2):
            h = [
                held[i * group : (i + 1) * group, part, pl.ds(pl.multiple_of(row + 16 * p, 16), 16)].reshape(
                    16 * group, LANES
                )
                for p in range(2)
            ]
            moved.append(jnp.dot(perm_ref[...], jnp.concatenate(h, axis=1), preferred_element_type=F32))
        return moved

    def turned_rows(n, i, t, g, moved):
        s0 = i * group + 8 * g
        angle = [[pair(n, part, a, s0, t) for part in range(2)] for a in range(2)]
        real, imag = [], []
        for e in range(8):
            c, s = angle[(e >> 1) & 1]
            at = ((t * 8 + e) * blocks + g) * 8
            x = moved[0][at : at + 8]
            y = moved[1][at : at + 8]
            real.append(c * x + s * y)
            imag.append(c * y - s * x)
        return real + imag

    def work(j, near):
        items = [(n, i) for n in range(chunk // WIDE) for i in range(steps // group)]
        sums = {}
        buf = j % 2

        def contract(n, i, ready):
            for t in range(2):
                top, low = ready[t]
                first = jnp.dot(k_ref[i], top, preferred_element_type=F32)
                second = jnp.dot(k_ref[i, :16], low, preferred_element_type=F32)
                if i > 0:
                    first, second = sums[n, t][0] + first, sums[n, t][1] + second
                sums[n, t] = first, second
                if i == steps // group - 1:
                    total = (first[:16] + first[16:]) + second
                    local = spans(j, n)
                    out_ref[:, local[t]] = total[:, :LANES]
                    out_ref[:, local[t + 2]] = total[:, LANES:]

        moved = move(j, *items[0])
        waiting = None
        for at, (n, i) in enumerate(items):
            later = move(j, *items[at + 1]) if at + 1 < len(items) else None
            if waiting is not None:
                contract(*waiting)
            following = jnp.minimum(j * chunk + (n + 1) * WIDE, columns - WIDE)
            if i == 0:
                sum_phases(following)
            make_waves(following, n + 1, i)
            ready = []
            rows = slice(i * 16 * group, (i + 1) * 16 * group)
            for t in range(2):
                x = jnp.concatenate(
                    [row for g in range(blocks) for row in turned_rows(n, i, t, g, moved)], axis=0
                )
                kept[buf, rows, n * WIDE + t * LANES : n * WIDE + (t + 1) * LANES] = x[:, :LANES]
                kept[buf, rows, n * WIDE + (t + 2) * LANES : n * WIDE + (t + 3) * LANES] = x[:, LANES:]
                top = x.astype(BF)
                ready.append((top, (x - top.astype(F32)).astype(BF)))
            waiting = (n, i, ready)
            moved = later
            if i == steps // group - 1:
                copy_out(j, n, near).start()
        contract(*waiting)

    def span(first, last, near):
        @pl.loop(first, last)
        def _(j):
            copy_in(j).wait()

            @pl.when(j + 1 < count)
            def _():
                for a in range(2):
                    copy_energy(j + 1, a).wait()

            @pl.when(j >= 2)
            def _():
                for n in range(chunk // WIDE):
                    copy_out(j, n, near).wait()

            work(j, near)

    perm_ref[...] = permutation()
    tri_ref[...] = suffix_rows(steps)
    for a in range(2):
        copy_energy(0, a).wait()
    sum_phases(0)
    for i in range(steps // group):
        make_waves(0, 0, i)
    span(0, inside, True)
    span(inside, count, False)
    for j in range(max(count - 2, 0), count):
        for n in range(chunk // WIDE):
            copy_out(j, n, j < inside).wait()


def predict(side, edge, weights, stored, energy, off):
    steps, columns = energy.shape[0], energy.shape[2] // 2
    group = GROUP
    chunk = min(CHUNK, columns)
    count = columns // chunk
    inside = count // 2
    size = steps * 16 * columns
    return pl.pallas_call(
        functools.partial(predict_kernel, inside, steps, group),
        in_specs=[SM, VM, HB, HB, VM],
        out_specs=[VM, HB, HB],
        out_shape=[jax.ShapeDtypeStruct((16, columns), F32)]
        + [jax.ShapeDtypeStruct((steps * 16, c), F32) for c in (inside * chunk, columns - inside * chunk)],
        scratch_shapes=[
            pltpu.VMEM((steps, 2, columns // 16, LANES), BF),
            pltpu.SemaphoreType.DMA((count,)),
            pltpu.VMEM((2, steps, columns), F32),
            pltpu.SemaphoreType.DMA((count, 2)),
            pltpu.VMEM((2, steps, WIDE), F32),
            pltpu.VMEM((2, 2, 2, steps, WIDE), F32),
            pltpu.VMEM((2, steps * 16, chunk), F32),
            pltpu.SemaphoreType.DMA((2, chunk // WIDE)),
            pltpu.VMEM((16 * group, 16 * group), BF),
            pltpu.VMEM((steps, 3 * steps), BF),
        ],
        compiler_params=pltpu.CompilerParams(vmem_limit_bytes=51 << 20),
        cost_estimate=pl.CostEstimate(flops=200 * size, bytes_accessed=6 * size, transcendentals=0),
        name="predict",
    )(
        jnp.stack([side, edge]).astype(jnp.int32),
        weights,
        stored,
        energy,
        off,
    )


def correct_kernel(inside, steps, group, sc_ref, k_ref, start_ref, pred_ref, *rest):
    near_ref = rest[0] if inside else None
    far_ref, out_ref, held, sems, wide_ref = rest[-5:]
    columns = out_ref.shape[-1]
    chunk = min(CHUNK, columns)
    count = columns // chunk
    width = 2 * LANES
    rows = 16 * group
    base = sc_ref[0] * columns

    def copy_in(j):
        lanes = pl.ds(pl.multiple_of(j * chunk, chunk), chunk)
        return pltpu.make_async_copy(far_ref.at[:, lanes], held.at[:, lanes], sems.at[j])

    for j in range(count - inside):
        copy_in(j).start()

    def work(j, source, offset):
        items = [(n, i) for n in range(chunk // width) for i in range(steps // group)]
        sums = {}

        def span(n):
            return pl.ds(pl.multiple_of(j * chunk + n * width, width), width)

        def contract(n, i, top, low):
            first = jnp.dot(k_ref[i], top, preferred_element_type=F32)
            second = jnp.dot(k_ref[i, :16], low, preferred_element_type=F32)
            if i > 0:
                first, second = sums[n][0] + first, sums[n][1] + second
            sums[n] = first, second
            if i == steps // group - 1:
                out_ref[:, span(n)] = (first[:16] + first[16:]) + second

        waiting = None
        for n, i in items:
            if waiting is not None:
                contract(*waiting)
            if i == 0:
                full = start_ref[:, pl.ds(pl.multiple_of(base + j * chunk + n * width, width), width)] + pred_ref[:, span(n)]
                full = 0.25 * full
                for c in range(16):
                    wide_ref[n, c] = jnp.broadcast_to(full[c : c + 1], (8, width))
            parts = []
            here = pl.ds(pl.multiple_of((j - offset) * chunk + n * width, width), width)
            for g in range(group // 8):
                at = i * rows + 128 * g
                turned = [source[at + 8 * c : at + 8 * c + 8, here] for c in range(16)]
                terms = [turned[c] * wide_ref[n, c] for c in range(16)]
                while len(terms) > 1:
                    terms = [terms[m] + terms[m + 1] for m in range(0, len(terms), 2)]
                vertex = 1.0 / (1.0 + terms[0] * terms[0])
                parts += [vertex * x for x in turned]
            x = jnp.concatenate(parts, axis=0)
            top = x.astype(BF)
            waiting = (n, i, top, (x - top.astype(F32)).astype(BF))
        contract(*waiting)

    if inside:

        @pl.loop(0, inside)
        def _(j):
            work(j, near_ref, 0)

    @pl.loop(inside, count)
    def _(j):
        copy_in(j - inside).wait()
        work(j, held, inside)


def correct(side, weights, start, pred, *turned):
    columns = pred.shape[1]
    steps = turned[0].shape[0] // 16
    group = GROUP
    chunk = min(CHUNK, columns)
    size = steps * 16 * columns
    far = turned[-1]
    inside = (columns - far.shape[1]) // chunk
    return pl.pallas_call(
        functools.partial(correct_kernel, inside, steps, group),
        in_specs=[SM, VM, VM, VM] + [VM] * (inside > 0) + [HB],
        out_specs=VM,
        out_shape=jax.ShapeDtypeStruct((16, columns), F32),
        scratch_shapes=[
            pltpu.VMEM(far.shape, F32),
            pltpu.SemaphoreType.DMA((columns // chunk - inside,)),
            pltpu.VMEM((chunk // (2 * LANES), 16, 8, 2 * LANES), F32),
        ],
        compiler_params=pltpu.CompilerParams(vmem_limit_bytes=44 << 20),
        cost_estimate=pl.CostEstimate(flops=120 * size, bytes_accessed=4 * size, transcendentals=0),
        name="correct",
    )(jnp.reshape(side, (1,)).astype(jnp.int32), weights, start, pred, *turned)


def carry_kernel(piece, stored_ref, *rest):
    new_ref, held, in_sems, out_sems = rest[-4:]
    steps = stored_ref.shape[0]
    each = held.shape[0]
    count = in_sems.shape[0]
    part = each // count

    def ends(p):
        here = held.at[pl.ds(p * part, part)]
        there = pl.ds(piece * each + p * part, part)
        read = pltpu.make_async_copy(stored_ref.at[there], here, in_sems.at[p])
        write = pltpu.make_async_copy(here, new_ref.at[there], out_sems.at[p])
        return read, write

    both = [ends(p) for p in range(count)]
    for read, _ in both:
        read.start()
    for read, write in both:
        read.wait()
        write.start()
    for _, write in both:
        write.wait()


def carry(piece, stored, new=None):
    steps = stored.shape[0]
    each = steps // pieces_of(steps)
    count = 4 if each % 4 == 0 else 1
    args = [stored] if new is None else [stored, new]
    size = 4 * stored.size // pieces_of(steps)
    return pl.pallas_call(
        functools.partial(carry_kernel, piece),
        in_specs=[HB] * len(args),
        out_specs=HB,
        out_shape=jax.ShapeDtypeStruct(stored.shape, stored.dtype),
        scratch_shapes=[
            pltpu.VMEM((each, *stored.shape[1:]), BF),
            pltpu.SemaphoreType.DMA((count,)),
            pltpu.SemaphoreType.DMA((count,)),
        ],
        input_output_aliases={} if new is None else {1: 0},
        compiler_params=pltpu.CompilerParams(vmem_limit_bytes=42 << 20),
        cost_estimate=pl.CostEstimate(flops=0, bytes_accessed=size, transcendentals=0),
        name="carry",
    )(*args)


def finish_kernel(sc_ref, old_ref, own_ref, other_ref, whole_ref, new_ref, held, sem, sems):
    half = own_ref.shape[1]
    side = sc_ref[0]
    places = ((side, own_ref), (1 - side, other_ref))
    writes = [
        pltpu.make_async_copy(ref, whole_ref.at[:, pl.ds(pl.multiple_of(at * half, LANES), half)], sems.at[n])
        for n, (at, ref) in enumerate(places)
    ]
    for write in writes:
        write.start()

    @pl.when(sc_ref[1] == 1)
    def _():
        for at, ref in places:
            for part in range(2):
                for n in range(half // (2 * LANES)):
                    tiles = [
                        ref[8 * part : 8 * part + 8, (2 * n + t) * LANES : (2 * n + t + 1) * LANES] for t in range(2)
                    ]
                    rows = pl.ds(pl.multiple_of(at * (half // 16) + 16 * n, 16), 16)
                    held[part, rows] = jnp.concatenate(tiles, axis=0).astype(BF)
        copy = pltpu.make_async_copy(held, new_ref.at[sc_ref[2]], sem)
        copy.start()
        copy.wait()

    for write in writes:
        write.wait()


def finish(side, own, slot, new, new_own, new_other):
    rows, half = new_own.shape
    return pl.pallas_call(
        finish_kernel,
        in_specs=[SM, HB, VM, VM],
        out_specs=[HB, HB],
        out_shape=[jax.ShapeDtypeStruct((rows, 2 * half), F32), jax.ShapeDtypeStruct(new.shape, new.dtype)],
        scratch_shapes=[
            pltpu.VMEM(new.shape[1:], BF),
            pltpu.SemaphoreType.DMA,
            pltpu.SemaphoreType.DMA((2,)),
        ],
        input_output_aliases={1: 1},
        compiler_params=pltpu.CompilerParams(vmem_limit_bytes=40 << 20),
        name="finish",
    )(jnp.stack([side, own, slot]).astype(jnp.int32), new, new_own, new_other)


def tiled(x):
    lead, columns = x.shape[:-2], x.shape[-1]
    x = x.reshape(*lead, 2, 8, columns // LANES, LANES)
    return jnp.swapaxes(x, -3, -2).reshape(*lead, 2, columns // 16, LANES)


def untiled(x):
    lead, rows = x.shape[:-3], x.shape[-2]
    x = jnp.swapaxes(x.reshape(*lead, 2, rows // 8, 8, LANES), -3, -2)
    return x.reshape(*lead, 16, rows * 16)


def rotate(values, angles):
    columns = angles.shape[-1]
    waves = half_sincos(0.5 * angles)
    s, c = [jnp.broadcast_to(x[None, :, None, :], (2, 2, 2, columns)).reshape(8, columns) for x in waves]
    real, imag = values[:8], values[8:]
    return jnp.concatenate([c * real + s * imag, c * imag - s * real], axis=0)


def on_device(history, energy, kernel, newest, current, step_energy):
    steps, _, columns = history.shape
    count = lax.axis_size("ta")
    place_here = lax.axis_index("ta")
    bits = count.bit_length() - 1
    half = columns // 2
    latest = newest[0]
    owner = lax.div(latest, steps)
    edge = latest - place_here * steps
    side = place_here & 1
    other = 1 - side

    def swap(x, mask):
        return lax.ppermute(x, "ta", [(i, i ^ mask) for i in range(count)])

    masks = [2] + [6 if t == 2 else 1 << t for t in range(2, bits)]
    split = (place_here >> 1 ^ place_here >> 2) & 1

    mine = place_here == owner
    value, late = totals(edge, energy)

    total, ahead = value, jnp.zeros_like(value)

    stored = tiled(history)
    new = None
    piece = 0

    def swaps_beside(sent, masks_):
        nonlocal new, piece
        if piece == pieces_of(steps):
            return [swap(x, mask) for x, mask in zip(sent, masks_)]
        sent, here = lax.optimization_barrier((sent, stored))
        got = [swap(x, mask) for x, mask in zip(sent, masks_)]
        got, new = lax.optimization_barrier((got, carry(piece, here, new)))
        piece += 1
        return got

    def counted(t, partner):
        here, there = place_here >> t, owner >> t
        beyond, within = partner > here, partner <= there
        between = jnp.where(here < there, beyond & within, beyond | within)
        return jnp.where(here == there, place_here >= owner, between)

    direct = bits == 3
    for t in range(1 if direct else bits):
        here, there = place_here >> t, owner >> t
        upper, partner = (here & 1) == 1, here ^ 1
        got = swap(total, 6 if t == 2 else 1 << t)
        ahead = ahead + jnp.where(counted(t, partner), got, 0.0)
        low_group = jnp.where(upper, partner, here)
        total = jnp.where(there == low_group, jnp.where(upper, got, total), total + got)
    if direct:
        for mask, got in zip((2, 4, 6), swaps_beside([total] * 3, (2, 4, 6))):
            ahead = ahead + jnp.where(counted(1, (place_here ^ mask) >> 1), got, 0.0)
    start = rotate(current, step_energy)
    off = 0.5 * jnp.stack([jnp.where(mine, -late, ahead), jnp.where(mine, ahead + value, ahead)])
    weights = kernel_rows(kernel)

    first = split == 0

    def inner_part(x, carried):
        keep = jnp.where(first, x[:8], x[8:])
        send = jnp.where(first, x[8:], x[:8])
        for n, mask in enumerate(masks):
            sent = keep if n else send
            (got,) = swaps_beside([sent], [mask]) if carried[min(n, 1)] else [swap(sent, mask)]
            keep = keep + got
        return keep

    def joined(keep, rest):
        return jnp.concatenate([jnp.where(first, keep, rest), jnp.where(first, rest, keep)], axis=0)

    part_other, *turned_other = predict(other, edge, weights, stored, energy, off)
    from_partner = swap(part_other, 1)
    part_own, *turned_own = predict(side, edge, weights, stored, energy, off)
    pred_own = inner_part(part_own + from_partner, (False, True))
    pred_own = joined(pred_own, swap(pred_own, masks[0]))
    pred_other = swap(pred_own, 1)
    corr_own = correct(side, weights, start, pred_own, *turned_own)
    from_partner = swap(corr_own, 1)
    corr_other = correct(other, weights, start, pred_other, *turned_other)
    def mine_of(x):
        x = jnp.where(side == 0, x[:, half:], x[:, :half]) if x.shape[1] > half else x
        return jnp.where(first, x[:8], x[8:])

    corr = inner_part(corr_other + from_partner, (True, True))
    fresh = mine_of(start) + 0.5 * (mine_of(pred_other) + corr)
    gathered = [swap(fresh, mask) for mask in (masks[0], masks[0] ^ 1, 1)]
    new_other = joined(fresh, gathered[0])
    new_own = joined(gathered[2], gathered[1])
    while piece < pieces_of(steps):
        new = carry(piece, stored, new)
        piece += 1
    target = lax.rem(latest + 1, steps * count)
    own = lax.div(target, steps) == place_here
    corrected, new = finish(side, own, lax.rem(target, steps), new, new_own, new_other)
    return corrected, untiled(new)


def solution(mesh):
    return jax.shard_map(
        on_device,
        mesh=mesh,
        in_specs=(
            P("ta", None, "ka"),
            P("ta", None, "ka"),
            P("ta", None, None),
            P(),
            P(None, "ka"),
            P(None, "ka"),
        ),
        out_specs=(P(None, "ka"), P("ta", None, "ka")),
        check_vma=False,
    )
```

```python
import functools

import jax
import jax.numpy as jnp
import numpy as np
from jax import lax
from jax.experimental import pallas as pl
from jax.experimental.pallas import tpu as pltpu
from jax.sharding import PartitionSpec as P

LANES = 128
WIDE = 4 * LANES
CHUNK = 1024
VM = pl.BlockSpec(memory_space=pltpu.VMEM)
SM = pl.BlockSpec(memory_space=pltpu.SMEM)
HB = pl.BlockSpec(memory_space=pltpu.HBM)
SIN = (1.41420874, -0.235676110, 0.0117467684, -2.59660918e-4)
COS = (1.41421350, -0.707105432, 0.0589211807, -1.95919014e-3, 3.27400865e-5)
BF = jnp.bfloat16
F32 = jnp.float32
SELF = [slice(t * LANES, (t + 1) * LANES) for t in range(4)]


GROUP = 8


def double_sincos(u):
    q = u * u
    z = u * (SIN[0] + q * (SIN[1] + q * (SIN[2] + q * SIN[3])))
    c = COS[0] + q * (COS[1] + q * (COS[2] + q * (COS[3] + q * COS[4])))
    return z * c, 1.0 - z * z


def half_sincos(half):
    turns = jnp.round(half * (1.0 / np.pi))
    return double_sincos((half - turns * 3.140625) - turns * 9.67653589793e-4)


def pieces_of(steps):
    return 4 if steps % 4 == 0 else 1


def totals_kernel(edge_ref, energy_ref, value_ref, late_ref, held, sems):
    steps = energy_ref.shape[0]
    pieces = pieces_of(steps)
    each = steps // pieces
    edge = edge_ref[0]

    def copy(p):
        part = pl.ds(p * each, each)
        return pltpu.make_async_copy(energy_ref.at[part], held.at[part], sems.at[p])

    for p in range(pieces):
        copy(p).start()
    total = jnp.zeros(value_ref.shape, F32)
    late = jnp.zeros(value_ref.shape, F32)
    for p in range(pieces):
        copy(p).wait()
        for s in range(p * each, (p + 1) * each):
            e = held[s]
            total = total + e
            late = late + e * (s > edge).astype(F32)
    mine = (edge >= 0) & (edge < steps)
    value_ref[...] = jnp.where(mine, total - late, total)
    late_ref[...] = late


def totals(edge, energy):
    steps, _, columns = energy.shape
    rows = columns // (LANES // 2)
    view = energy.reshape(steps, 2, columns // LANES, LANES).transpose(0, 2, 1, 3).reshape(steps, rows, LANES)
    return pl.pallas_call(
        totals_kernel,
        in_specs=[SM, HB],
        out_specs=[VM, VM],
        out_shape=[jax.ShapeDtypeStruct((rows, LANES), F32)] * 2,
        scratch_shapes=[pltpu.VMEM(view.shape, F32), pltpu.SemaphoreType.DMA((pieces_of(steps),))],
        compiler_params=pltpu.CompilerParams(vmem_limit_bytes=51 << 20),
        cost_estimate=pl.CostEstimate(flops=4 * energy.size, bytes_accessed=4 * energy.size, transcendentals=0),
        name="totals",
    )(jnp.reshape(edge, (1,)).astype(jnp.int32), view)


def suffix_rows(steps):
    row = lax.broadcasted_iota(jnp.int32, (steps, 3 * steps), 0)
    column = lax.rem(lax.broadcasted_iota(jnp.int32, (steps, 3 * steps), 1), steps)
    return jnp.where(column >= row, 0.5, 0.0).astype(BF)


def permutation():
    rows = 16 * GROUP
    row = lax.broadcasted_iota(jnp.int32, (rows, rows), 0)
    column = lax.broadcasted_iota(jnp.int32, (rows, rows), 1)
    return jnp.where(column == (row & (GROUP - 1)) * 16 + lax.div(row, GROUP), 1.0, 0.0).astype(BF)


def kernel_rows(kernel):
    steps = kernel.shape[0]
    group = GROUP
    k = kernel.reshape(steps // group, group // 8, 8, 16, 16).transpose(0, 3, 1, 4, 2)
    k = k.reshape(steps // group, 16, 16 * group)
    top = lax.reduce_precision(k, 8, 7)
    return jnp.concatenate([top, k - top], axis=1).astype(BF)


def predict_kernel(inside, steps, group, sc_ref, k_ref, h_ref, energy_ref, off_ref, out_ref, *rest):
    near_ref, far_ref, held, in_sems, energies, energy_sems, halves, waves, kept, out_sems, perm_ref, tri_ref = rest
    columns = out_ref.shape[-1]
    chunk = kept.shape[-1]
    count = columns // chunk
    tiles = chunk // LANES
    blocks = group // 8
    edge = sc_ref[1]

    def copy_in(j, n):
        row = (j * tiles + 4 * n) * 8
        there = pl.ds(pl.multiple_of(sc_ref[0] * (columns // LANES) * 8 + row, 32), 32)
        here = pl.ds(pl.multiple_of(row, 32), 32)
        return pltpu.make_async_copy(h_ref.at[:, :, there], held.at[:, :, here], in_sems.at[j, n])

    def copy_out(j, n, near):
        there = pl.ds(pl.multiple_of((j if near else j - inside) * chunk + n * WIDE, WIDE), WIDE)
        here = kept.at[j % 2, :, pl.ds(n * WIDE, WIDE)]
        return pltpu.make_async_copy(here, (near_ref if near else far_ref).at[:, there], out_sems.at[j % 2, n])

    def copy_energy(j, a):
        there = pl.ds(pl.multiple_of(sc_ref[0] * columns + j * chunk, chunk), chunk)
        here = pl.ds(pl.multiple_of(j * chunk, chunk), chunk)
        return pltpu.make_async_copy(energy_ref.at[:, a, there], energies.at[a, :, here], energy_sems.at[j, a])

    for j in range(count):
        for a in range(2):
            copy_energy(j, a).start()
        for n in range(chunk // WIDE):
            copy_in(j, n).start()

    def spans(j, n):
        first = j * chunk + n * WIDE
        local = [pl.ds(pl.multiple_of(first + LANES * t, LANES), LANES) for t in range(4)]
        return local

    def pair(n, part, a, s0, t):
        both = [waves[n % 2, part, a, s0 : s0 + 8, LANES * m : LANES * (m + 1)] for m in (t, t + 2)]
        return jnp.concatenate(both, axis=-1)

    def sum_phases(first):
        for a in range(2):
            e = energies[a, :, pl.ds(pl.multiple_of(first, WIDE), WIDE)]
            top = e.astype(BF)
            rest = e - top.astype(F32)
            mid = rest.astype(BF)
            low = (rest - mid.astype(F32)).astype(BF)
            parts = jnp.concatenate([top, mid, low], axis=0)
            halves[a] = jnp.dot(tri_ref[...], parts, preferred_element_type=F32)

    def make_waves(first, n, i):
        after = lax.broadcasted_iota(jnp.int32, (group, WIDE), 0) + i * group > edge
        tile = sc_ref[0] * (columns // LANES) + lax.div(first, LANES)
        rows = slice(i * group, (i + 1) * group)
        for a in range(2):
            low, up = [
                jnp.concatenate([off_ref[later, pl.ds(2 * (tile + t) + a, 1)] for t in range(4)], axis=-1)
                for later in range(2)
            ]
            s, c = half_sincos(halves[a, rows] + jnp.where(after, up, low))
            waves[n % 2, 0, a, rows] = c
            waves[n % 2, 1, a, rows] = s

    def move(j, n, i):
        row = pl.multiple_of(j * tiles * 8 + n * 32, 16)
        moved = []
        for part in range(2):
            h = [
                held[i * group : (i + 1) * group, part, pl.ds(pl.multiple_of(row + 16 * p, 16), 16)].reshape(
                    16 * group, LANES
                )
                for p in range(2)
            ]
            moved.append(jnp.dot(perm_ref[...], jnp.concatenate(h, axis=1), preferred_element_type=F32))
        return moved

    def turned_rows(n, i, t, g, moved):
        s0 = i * group + 8 * g
        angle = [[pair(n, part, a, s0, t) for part in range(2)] for a in range(2)]
        real, imag = [], []
        for e in range(8):
            c, s = angle[(e >> 1) & 1]
            at = ((t * 8 + e) * blocks + g) * 8
            x = moved[0][at : at + 8]
            y = moved[1][at : at + 8]
            real.append(c * x + s * y)
            imag.append(c * y - s * x)
        return real + imag

    def work(j, near):
        items = [(n, i) for n in range(chunk // WIDE) for i in range(steps // group)]
        sums = {}
        buf = j % 2

        def contract(n, i, ready):
            for t in range(2):
                top, low = ready[t]
                first = jnp.dot(k_ref[i], top, preferred_element_type=F32)
                second = jnp.dot(k_ref[i, :16], low, preferred_element_type=F32)
                if i > 0:
                    first, second = sums[n, t][0] + first, sums[n, t][1] + second
                sums[n, t] = first, second
                if i == steps // group - 1:
                    total = (first[:16] + first[16:]) + second
                    local = spans(j, n)
                    out_ref[:, local[t]] = total[:, :LANES]
                    out_ref[:, local[t + 2]] = total[:, LANES:]

        copy_in(j, 0).wait()
        moved = move(j, *items[0])
        waiting = None
        for at, (n, i) in enumerate(items):
            if at + 1 < len(items) and items[at + 1][1] == 0:
                copy_in(j, n + 1).wait()
            later = move(j, *items[at + 1]) if at + 1 < len(items) else None
            if waiting is not None:
                contract(*waiting)
            following = jnp.minimum(j * chunk + (n + 1) * WIDE, columns - WIDE)
            if i == 0:
                sum_phases(following)
            make_waves(following, n + 1, i)
            ready = []
            rows = slice(i * 16 * group, (i + 1) * 16 * group)
            for t in range(2):
                x = jnp.concatenate(
                    [row for g in range(blocks) for row in turned_rows(n, i, t, g, moved)], axis=0
                )
                kept[buf, rows, n * WIDE + t * LANES : n * WIDE + (t + 1) * LANES] = x[:, :LANES]
                kept[buf, rows, n * WIDE + (t + 2) * LANES : n * WIDE + (t + 3) * LANES] = x[:, LANES:]
                top = x.astype(BF)
                ready.append((top, (x - top.astype(F32)).astype(BF)))
            waiting = (n, i, ready)
            moved = later
            if i == steps // group - 1:
                copy_out(j, n, near).start()
        contract(*waiting)

    def span(first, last, near):
        @pl.loop(first, last)
        def _(j):
            @pl.when(j + 1 < count)
            def _():
                for a in range(2):
                    copy_energy(j + 1, a).wait()

            @pl.when(j >= 2)
            def _():
                for n in range(chunk // WIDE):
                    copy_out(j, n, near).wait()

            work(j, near)

    perm_ref[...] = permutation()
    tri_ref[...] = suffix_rows(steps)
    for a in range(2):
        copy_energy(0, a).wait()
    sum_phases(0)
    for i in range(steps // group):
        make_waves(0, 0, i)
    span(0, inside, True)
    span(inside, count, False)
    for j in range(max(count - 2, 0), count):
        for n in range(chunk // WIDE):
            copy_out(j, n, j < inside).wait()


def predict(side, edge, weights, stored, energy, off):
    steps, columns = energy.shape[0], energy.shape[2] // 2
    group = GROUP
    chunk = min(CHUNK, columns)
    count = columns // chunk
    inside = count // 2
    size = steps * 16 * columns
    return pl.pallas_call(
        functools.partial(predict_kernel, inside, steps, group),
        in_specs=[SM, VM, HB, HB, VM],
        out_specs=[VM, HB, HB],
        out_shape=[jax.ShapeDtypeStruct((16, columns), F32)]
        + [jax.ShapeDtypeStruct((steps * 16, c), F32) for c in (inside * chunk, columns - inside * chunk)],
        scratch_shapes=[
            pltpu.VMEM((steps, 2, columns // 16, LANES), BF),
            pltpu.SemaphoreType.DMA((count, chunk // WIDE)),
            pltpu.VMEM((2, steps, columns), F32),
            pltpu.SemaphoreType.DMA((count, 2)),
            pltpu.VMEM((2, steps, WIDE), F32),
            pltpu.VMEM((2, 2, 2, steps, WIDE), F32),
            pltpu.VMEM((2, steps * 16, chunk), F32),
            pltpu.SemaphoreType.DMA((2, chunk // WIDE)),
            pltpu.VMEM((16 * group, 16 * group), BF),
            pltpu.VMEM((steps, 3 * steps), BF),
        ],
        compiler_params=pltpu.CompilerParams(vmem_limit_bytes=51 << 20),
        cost_estimate=pl.CostEstimate(flops=200 * size, bytes_accessed=6 * size, transcendentals=0),
        name="predict",
    )(
        jnp.stack([side, edge]).astype(jnp.int32),
        weights,
        stored,
        energy,
        off,
    )


def correct_kernel(inside, steps, group, sc_ref, k_ref, start_ref, pred_ref, *rest):
    near_ref = rest[0] if inside else None
    far_ref, out_ref, held, sems, wide_ref = rest[-5:]
    columns = out_ref.shape[-1]
    chunk = min(CHUNK, columns)
    count = columns // chunk
    width = 2 * LANES
    rows = 16 * group
    base = sc_ref[0] * columns

    def copy_in(j):
        lanes = pl.ds(pl.multiple_of(j * chunk, chunk), chunk)
        return pltpu.make_async_copy(far_ref.at[:, lanes], held.at[:, lanes], sems.at[j])

    for j in range(count - inside):
        copy_in(j).start()

    def work(j, source, offset):
        items = [(n, i) for n in range(chunk // width) for i in range(steps // group)]
        sums = {}

        def span(n):
            return pl.ds(pl.multiple_of(j * chunk + n * width, width), width)

        def contract(n, i, top, low):
            first = jnp.dot(k_ref[i], top, preferred_element_type=F32)
            second = jnp.dot(k_ref[i, :16], low, preferred_element_type=F32)
            if i > 0:
                first, second = sums[n][0] + first, sums[n][1] + second
            sums[n] = first, second
            if i == steps // group - 1:
                out_ref[:, span(n)] = (first[:16] + first[16:]) + second

        waiting = None
        for n, i in items:
            if waiting is not None:
                contract(*waiting)
            if i == 0:
                full = start_ref[:, pl.ds(pl.multiple_of(base + j * chunk + n * width, width), width)] + pred_ref[:, span(n)]
                full = 0.25 * full
                for c in range(16):
                    wide_ref[n, c] = jnp.broadcast_to(full[c : c + 1], (8, width))
            parts = []
            here = pl.ds(pl.multiple_of((j - offset) * chunk + n * width, width), width)
            for g in range(group // 8):
                at = i * rows + 128 * g
                turned = [source[at + 8 * c : at + 8 * c + 8, here] for c in range(16)]
                terms = [turned[c] * wide_ref[n, c] for c in range(16)]
                while len(terms) > 1:
                    terms = [terms[m] + terms[m + 1] for m in range(0, len(terms), 2)]
                vertex = 1.0 / (1.0 + terms[0] * terms[0])
                parts += [vertex * x for x in turned]
            x = jnp.concatenate(parts, axis=0)
            top = x.astype(BF)
            waiting = (n, i, top, (x - top.astype(F32)).astype(BF))
        contract(*waiting)

    if inside:

        @pl.loop(0, inside)
        def _(j):
            work(j, near_ref, 0)

    @pl.loop(inside, count)
    def _(j):
        copy_in(j - inside).wait()
        work(j, held, inside)


def correct(side, weights, start, pred, *turned):
    columns = pred.shape[1]
    steps = turned[0].shape[0] // 16
    group = GROUP
    chunk = min(CHUNK, columns)
    size = steps * 16 * columns
    far = turned[-1]
    inside = (columns - far.shape[1]) // chunk
    return pl.pallas_call(
        functools.partial(correct_kernel, inside, steps, group),
        in_specs=[SM, VM, VM, VM] + [VM] * (inside > 0) + [HB],
        out_specs=VM,
        out_shape=jax.ShapeDtypeStruct((16, columns), F32),
        scratch_shapes=[
            pltpu.VMEM(far.shape, F32),
            pltpu.SemaphoreType.DMA((columns // chunk - inside,)),
            pltpu.VMEM((chunk // (2 * LANES), 16, 8, 2 * LANES), F32),
        ],
        compiler_params=pltpu.CompilerParams(vmem_limit_bytes=44 << 20),
        cost_estimate=pl.CostEstimate(flops=120 * size, bytes_accessed=4 * size, transcendentals=0),
        name="correct",
    )(jnp.reshape(side, (1,)).astype(jnp.int32), weights, start, pred, *turned)


def carry_kernel(piece, stored_ref, *rest):
    new_ref, held, in_sems, out_sems = rest[-4:]
    steps = stored_ref.shape[0]
    each = held.shape[0]
    count = in_sems.shape[0]
    part = each // count

    def ends(p):
        here = held.at[pl.ds(p * part, part)]
        there = pl.ds(piece * each + p * part, part)
        read = pltpu.make_async_copy(stored_ref.at[there], here, in_sems.at[p])
        write = pltpu.make_async_copy(here, new_ref.at[there], out_sems.at[p])
        return read, write

    both = [ends(p) for p in range(count)]
    for read, _ in both:
        read.start()
    for read, write in both:
        read.wait()
        write.start()
    for _, write in both:
        write.wait()


def carry(piece, stored, new=None):
    steps = stored.shape[0]
    each = steps // pieces_of(steps)
    count = 4 if each % 4 == 0 else 1
    args = [stored] if new is None else [stored, new]
    size = 4 * stored.size // pieces_of(steps)
    return pl.pallas_call(
        functools.partial(carry_kernel, piece),
        in_specs=[HB] * len(args),
        out_specs=HB,
        out_shape=jax.ShapeDtypeStruct(stored.shape, stored.dtype),
        scratch_shapes=[
            pltpu.VMEM((each, *stored.shape[1:]), BF),
            pltpu.SemaphoreType.DMA((count,)),
            pltpu.SemaphoreType.DMA((count,)),
        ],
        input_output_aliases={} if new is None else {1: 0},
        compiler_params=pltpu.CompilerParams(vmem_limit_bytes=42 << 20),
        cost_estimate=pl.CostEstimate(flops=0, bytes_accessed=size, transcendentals=0),
        name="carry",
    )(*args)


def finish_kernel(sc_ref, old_ref, own_ref, other_ref, whole_ref, new_ref, held, sem, sems):
    half = own_ref.shape[1]
    side = sc_ref[0]
    places = ((side, own_ref), (1 - side, other_ref))
    writes = [
        pltpu.make_async_copy(ref, whole_ref.at[:, pl.ds(pl.multiple_of(at * half, LANES), half)], sems.at[n])
        for n, (at, ref) in enumerate(places)
    ]
    for write in writes:
        write.start()

    @pl.when(sc_ref[1] == 1)
    def _():
        for at, ref in places:
            for part in range(2):
                for n in range(half // (2 * LANES)):
                    tiles = [
                        ref[8 * part : 8 * part + 8, (2 * n + t) * LANES : (2 * n + t + 1) * LANES] for t in range(2)
                    ]
                    rows = pl.ds(pl.multiple_of(at * (half // 16) + 16 * n, 16), 16)
                    held[part, rows] = jnp.concatenate(tiles, axis=0).astype(BF)
        copy = pltpu.make_async_copy(held, new_ref.at[sc_ref[2]], sem)
        copy.start()
        copy.wait()

    for write in writes:
        write.wait()


def finish(side, own, slot, new, new_own, new_other):
    rows, half = new_own.shape
    return pl.pallas_call(
        finish_kernel,
        in_specs=[SM, HB, VM, VM],
        out_specs=[HB, HB],
        out_shape=[jax.ShapeDtypeStruct((rows, 2 * half), F32), jax.ShapeDtypeStruct(new.shape, new.dtype)],
        scratch_shapes=[
            pltpu.VMEM(new.shape[1:], BF),
            pltpu.SemaphoreType.DMA,
            pltpu.SemaphoreType.DMA((2,)),
        ],
        input_output_aliases={1: 1},
        compiler_params=pltpu.CompilerParams(vmem_limit_bytes=40 << 20),
        name="finish",
    )(jnp.stack([side, own, slot]).astype(jnp.int32), new, new_own, new_other)


def tiled(x):
    lead, columns = x.shape[:-2], x.shape[-1]
    x = x.reshape(*lead, 2, 8, columns // LANES, LANES)
    return jnp.swapaxes(x, -3, -2).reshape(*lead, 2, columns // 16, LANES)


def untiled(x):
    lead, rows = x.shape[:-3], x.shape[-2]
    x = jnp.swapaxes(x.reshape(*lead, 2, rows // 8, 8, LANES), -3, -2)
    return x.reshape(*lead, 16, rows * 16)


def rotate(values, angles):
    columns = angles.shape[-1]
    waves = half_sincos(0.5 * angles)
    s, c = [jnp.broadcast_to(x[None, :, None, :], (2, 2, 2, columns)).reshape(8, columns) for x in waves]
    real, imag = values[:8], values[8:]
    return jnp.concatenate([c * real + s * imag, c * imag - s * real], axis=0)


def on_device(history, energy, kernel, newest, current, step_energy):
    steps, _, columns = history.shape
    count = lax.axis_size("ta")
    place_here = lax.axis_index("ta")
    bits = count.bit_length() - 1
    half = columns // 2
    latest = newest[0]
    owner = lax.div(latest, steps)
    edge = latest - place_here * steps
    side = place_here & 1
    other = 1 - side

    def swap(x, mask):
        return lax.ppermute(x, "ta", [(i, i ^ mask) for i in range(count)])

    masks = [2] + [6 if t == 2 else 1 << t for t in range(2, bits)]
    split = (place_here >> 1 ^ place_here >> 2) & 1

    mine = place_here == owner
    value, late = totals(edge, energy)

    total, ahead = value, jnp.zeros_like(value)

    stored = tiled(history)
    new = None
    piece = 0

    def swaps_beside(sent, masks_):
        nonlocal new, piece
        if piece == pieces_of(steps):
            return [swap(x, mask) for x, mask in zip(sent, masks_)]
        sent, here = lax.optimization_barrier((sent, stored))
        got = [swap(x, mask) for x, mask in zip(sent, masks_)]
        got, new = lax.optimization_barrier((got, carry(piece, here, new)))
        piece += 1
        return got

    def counted(t, partner):
        here, there = place_here >> t, owner >> t
        beyond, within = partner > here, partner <= there
        between = jnp.where(here < there, beyond & within, beyond | within)
        return jnp.where(here == there, place_here >= owner, between)

    direct = bits == 3
    for t in range(1 if direct else bits):
        here, there = place_here >> t, owner >> t
        upper, partner = (here & 1) == 1, here ^ 1
        got = swap(total, 6 if t == 2 else 1 << t)
        ahead = ahead + jnp.where(counted(t, partner), got, 0.0)
        low_group = jnp.where(upper, partner, here)
        total = jnp.where(there == low_group, jnp.where(upper, got, total), total + got)
    if direct:
        for mask, got in zip((2, 4, 6), swaps_beside([total] * 3, (2, 4, 6))):
            ahead = ahead + jnp.where(counted(1, (place_here ^ mask) >> 1), got, 0.0)
    start = rotate(current, step_energy)
    off = 0.5 * jnp.stack([jnp.where(mine, -late, ahead), jnp.where(mine, ahead + value, ahead)])
    weights = kernel_rows(kernel)

    first = split == 0

    def inner_part(x, carried):
        keep = jnp.where(first, x[:8], x[8:])
        send = jnp.where(first, x[8:], x[:8])
        for n, mask in enumerate(masks):
            sent = keep if n else send
            (got,) = swaps_beside([sent], [mask]) if carried[min(n, 1)] else [swap(sent, mask)]
            keep = keep + got
        return keep

    def joined(keep, rest):
        return jnp.concatenate([jnp.where(first, keep, rest), jnp.where(first, rest, keep)], axis=0)

    part_other, *turned_other = predict(other, edge, weights, stored, energy, off)
    from_partner = swap(part_other, 1)
    part_own, *turned_own = predict(side, edge, weights, stored, energy, off)
    pred_own = inner_part(part_own + from_partner, (False, True))
    pred_own = joined(pred_own, swap(pred_own, masks[0]))
    pred_other = swap(pred_own, 1)
    corr_own = correct(side, weights, start, pred_own, *turned_own)
    from_partner = swap(corr_own, 1)
    corr_other = correct(other, weights, start, pred_other, *turned_other)
    def mine_of(x):
        x = jnp.where(side == 0, x[:, half:], x[:, :half]) if x.shape[1] > half else x
        return jnp.where(first, x[:8], x[8:])

    corr = inner_part(corr_other + from_partner, (True, True))
    fresh = mine_of(start) + 0.5 * (mine_of(pred_other) + corr)
    gathered = [swap(fresh, mask) for mask in (masks[0], masks[0] ^ 1, 1)]
    new_other = joined(fresh, gathered[0])
    new_own = joined(gathered[2], gathered[1])
    while piece < pieces_of(steps):
        new = carry(piece, stored, new)
        piece += 1
    target = lax.rem(latest + 1, steps * count)
    own = lax.div(target, steps) == place_here
    corrected, new = finish(side, own, lax.rem(target, steps), new, new_own, new_other)
    return corrected, untiled(new)


def solution(mesh):
    return jax.shard_map(
        on_device,
        mesh=mesh,
        in_specs=(
            P("ta", None, "ka"),
            P("ta", None, "ka"),
            P("ta", None, None),
            P(),
            P(None, "ka"),
            P(None, "ka"),
        ),
        out_specs=(P(None, "ka"), P("ta", None, "ka")),
        check_vma=False,
    )
```
